256 devices in a mesh: ctx: 64 (over y, z, core), kvh: 4 (over x).
Axes of the slice: x: 4, y: 4, z: 8, core: 2. Of those that a mesh axis runs over, the one named last changes fastest.
Arguments:
- queries: bfloat16 [256, 64, 128], P('ctx', 'kvh'), may hold values from -30 to 30
- span_keys: bfloat16 [256, 8, 128], P('ctx', 'kvh'), may hold values from -16 to 16
- span_values: bfloat16 [256, 8, 128], P('ctx', 'kvh'), may hold values from -12 to 12
- cache_keys: bfloat16 [524288, 8, 128], P('ctx', 'kvh'), may hold values from -16 to 16
- cache_values: bfloat16 [524288, 8, 128], P('ctx', 'kvh'), may hold values from -7 to 7
- gating: int32 [64, 12], P('kvh'), may hold values from 0 to 127, all different within a row; in each aligned block of 16 rows (0 to 15, 16 to 31, ...) at most 3 rows name the same one
- out_weight: bfloat16 [8192, 8192], P('kvh', 'ctx'), may hold values from -0.0625 to 0.0625
Outputs:
- attended: bfloat16 [256, 64, 128], P('ctx', 'kvh')
- projected: bfloat16 [256, 8192], P('kvh', 'ctx')
The draws below stay inside these ranges and needn't reach their ends.
Inputs may be any that keep to these rules, and one draw needn't show every extreme that they name: `gating`: each row names 12 distinct blocks. Among the heads of one index of kvh no block is named by more than 3 heads, and some block is named by exactly 3.
All inputs are finite; a program needn't handle non-finite values.
Results may differ from the reference program's by a relative error of at most 0.015.
Values may be sent and summed in bfloat16 or wider, within the bound.
A program may use at most 128 MiB of HBM per device.

```python
import math
import jax
import jax.numpy as jnp
import numpy as np
from jax import lax

QUERY_HEADS = 64
KEY_VALUE_HEADS = 8
HEAD_SIZE = 128
D = 8192
BLOCK_POSITIONS = 4096
TOPK = 12
CONTEXT_BLOCKS = 128
NEW_POSITIONS = 256
MOST = 3
N_KVH = 4


def draw_queries(key, part):
    key = jax.random.fold_in(key, 11)
    leading_part = jax.random.fold_in(key, 0)
    starting_point = jax.random.truncated_normal(leading_part, -6.0, 6.0, (NEW_POSITIONS, QUERY_HEADS, HEAD_SIZE), jnp.float32)
    return starting_point.astype(jnp.bfloat16)


def draw_cache_keys(key, part):
    key = jax.random.fold_in(key, 23)
    leading_part = jax.random.fold_in(key, 0)
    starting_point = jax.random.truncated_normal(leading_part, -6.0, 6.0, (CONTEXT_BLOCKS * BLOCK_POSITIONS, KEY_VALUE_HEADS, HEAD_SIZE), jnp.float32)
    return starting_point.astype(jnp.bfloat16)


def draw_span_keys(key, part):
    key = jax.random.fold_in(key, 37)
    leading_part = jax.random.fold_in(key, 0)
    starting_point = jax.random.truncated_normal(leading_part, -6.0, 6.0, (NEW_POSITIONS, KEY_VALUE_HEADS, HEAD_SIZE), jnp.float32)
    return starting_point.astype(jnp.bfloat16)


def draw_cache_values(key, part):
    key = jax.random.fold_in(key, 41)
    leading_part, trailing_part = jax.random.split(key)
    starting_point = jax.random.truncated_normal(leading_part, -6.0, 6.0, (CONTEXT_BLOCKS, BLOCK_POSITIONS, KEY_VALUE_HEADS, HEAD_SIZE), jnp.float32)
    position_shift = jax.random.truncated_normal(trailing_part, -4.0, 4.0, (CONTEXT_BLOCKS, 1, KEY_VALUE_HEADS, HEAD_SIZE), jnp.float32)
    return (0.5 * starting_point + position_shift).reshape(CONTEXT_BLOCKS * BLOCK_POSITIONS, KEY_VALUE_HEADS, HEAD_SIZE).astype(jnp.bfloat16)


def draw_span_values(key, part):
    key = jax.random.fold_in(key, 53)
    leading_part, trailing_part = jax.random.split(key)
    starting_point = jax.random.truncated_normal(leading_part, -3.0, 3.0, (NEW_POSITIONS, KEY_VALUE_HEADS, HEAD_SIZE), jnp.float32)
    position_shift = jax.random.truncated_normal(trailing_part, -3.0, 3.0, (1, KEY_VALUE_HEADS, HEAD_SIZE), jnp.float32)
    return (starting_point + 3.0 * position_shift).astype(jnp.bfloat16)


def shard_levels(key, extent, shards, low, high):
    factor_of, own = 1.0, jax.random.fold_in(key, 6)
    for dim, parts in shards:
        heights = jnp.exp(jax.random.uniform(jax.random.fold_in(own, dim), (parts,), jnp.float32, low / len(shards), high / len(shards)))
        factor_of = factor_of * jnp.repeat(heights, extent[dim] // parts).reshape([-1 if axis == dim else 1 for axis in range(len(extent))])
    return factor_of


def routed_block(rng, own, number, rows, number_of, top, bound, skew):
    sequence = jax.random.permutation(rng, number_of)
    crowded, ordinary = load_shares(number_of, rows * top, bound, skew, True), load_shares(number_of, rows * top, bound, skew, False)
    places = jnp.arange(number_of)

    def named(tallies, rotation):
        used = int((tallies > 0).sum())
        fixed = max(1, used // 4)
        moved = fixed + (places - fixed + rotation * (used - fixed)) % max(1, number_of - fixed)
        return jnp.zeros((number_of,), jnp.int32).at[sequence[jnp.where(places < fixed, places, moved)]].set(jnp.asarray(tallies, jnp.int32))

    tallies = jnp.where(number % 4 == 0, named(crowded, number // 4), named(ordinary, number - number // 4 - 1))
    mixed = jax.random.permutation(jax.random.fold_in(own, 3), number_of)
    giver, taker = mixed[0:number_of // 2 * 2:2], mixed[1:number_of // 2 * 2:2]
    slack = jnp.minimum(tallies[giver] - 1, bound - tallies[taker]) // 2
    slack = jnp.where((giver == sequence[0]) | (taker == sequence[0]) | (tallies[taker] == 0), 0, jnp.maximum(slack, 0))
    moved = jax.random.randint(jax.random.fold_in(own, 4), (number_of // 2,), 0, 1 << 20) % (slack + 1)
    tallies = tallies.at[giver].add(-moved).at[taker].add(moved)
    members = jnp.searchsorted(jnp.cumsum(tallies), jnp.arange(rows * top), side="right").astype(jnp.int32)
    listing = members.reshape(top, rows).T
    listing = listing[jax.random.permutation(jax.random.fold_in(own, 1), rows)]
    rotation = jax.random.randint(jax.random.fold_in(own, 2), (rows, 1), 0, top)
    return jnp.take_along_axis(listing, (jnp.arange(top)[None, :] + rotation) % top, axis=1)


def load_shares(number_of, total, bound, slope, full):
    loads = [(1 << 20) // math.isqrt(grade ** slope) + 1 for grade in range(1, number_of + 1)]
    largest = bound if full else min(bound, max(-(-total // number_of), total * loads[0] // sum(loads)))
    least = 1 if total - largest >= number_of - 1 else 0
    given, spare = [largest] + [least] * (number_of - 1), total - largest - least * (number_of - 1)
    while spare > 0:
        free = [i for i in range(1, number_of) if given[i] < largest] or [i for i in range(1, number_of) if given[i] < bound]
        whole, remaining = sum([loads[i] for i in free]), spare
        for i in free:
            more = min(bound - given[i], max(1, remaining * loads[i] // whole), spare)
            given[i] = given[i] + more
            spare = spare - more
    return np.array(given)


def gaussian(rng, shape, spread, most, cuts=(), kind=jnp.bfloat16):
    drawn = spread * jax.random.normal(rng, shape, jnp.float32)
    if cuts:
        drawn = drawn * shard_levels(rng, shape, cuts, -0.22, 0.18)
    return jnp.clip(drawn, -most, most).astype(kind)


def setup_inputs(seed: int = 0) -> dict:
    key_of = jax.random.split(jax.random.key(seed), 8)
    queries = draw_queries(jax.random.fold_in(key_of[7], 71), 0)
    span_keys = draw_span_keys(jax.random.fold_in(key_of[7], 71), 0)
    span_values = draw_span_values(jax.random.fold_in(key_of[7], 71), 0)
    cache_keys = draw_cache_keys(jax.random.fold_in(key_of[7], 71), 0)
    cache_values = draw_cache_values(jax.random.fold_in(key_of[7], 71), 0)
    gating_keys = jax.random.split(jax.random.fold_in(key_of[5], 1), QUERY_HEADS // (QUERY_HEADS // N_KVH))
    gating_turns = jax.random.permutation(jax.random.fold_in(key_of[5], 3), QUERY_HEADS // (QUERY_HEADS // N_KVH))
    gating = jax.vmap(lambda own, number: routed_block(jax.random.fold_in(key_of[5], 2), own, number, QUERY_HEADS // N_KVH, CONTEXT_BLOCKS, TOPK, MOST, 2))(gating_keys, gating_turns).reshape((QUERY_HEADS, TOPK))
    out_weight = gaussian(key_of[6], (QUERY_HEADS * HEAD_SIZE, D), (QUERY_HEADS * HEAD_SIZE) ** -0.5, 0.0625, ((0, 4), (1, 64)))
    return dict(queries=queries, span_keys=span_keys, span_values=span_values, cache_keys=cache_keys, cache_values=cache_values, gating=gating, out_weight=out_weight)


NEG = -1e30


def block_partial(query, keys, values, scale):
    scores = jnp.dot(query, keys.T, preferred_element_type=jnp.float32) * scale
    top = jnp.max(scores, axis=1)
    weights = jnp.exp(scores - top[:, None])
    total = jnp.sum(weights, axis=1)
    out = jnp.dot(weights.astype(jnp.bfloat16), values, preferred_element_type=jnp.float32)
    return top, total, out


def reference(queries, span_keys, span_values, cache_keys, cache_values, gating, out_weight):
    scale = HEAD_SIZE ** -0.5
    group_factor = QUERY_HEADS // KEY_VALUE_HEADS
    positions = jnp.arange(NEW_POSITIONS, dtype=jnp.int32)
    causal = positions[None, :] <= positions[:, None]

    def one_head(head):
        group = head // group_factor
        query = lax.dynamic_index_in_dim(queries, head, 1, False)
        own_keys = lax.dynamic_index_in_dim(span_keys, group, 1, False)
        own_values = lax.dynamic_index_in_dim(span_values, group, 1, False)
        own_scores = jnp.dot(query, own_keys.T, preferred_element_type=jnp.float32) * scale
        own_scores = jnp.where(causal, own_scores, NEG)
        own_max = jnp.max(own_scores, axis=1)
        own_weights = jnp.where(causal, jnp.exp(own_scores - own_max[:, None]), 0.0)
        own_total = jnp.sum(own_weights, axis=1)
        own_out = jnp.dot(own_weights.astype(jnp.bfloat16), own_values, preferred_element_type=jnp.float32)
        chosen = lax.dynamic_index_in_dim(gating, head, 0, False)

        def step(carry, block):
            start = (block * BLOCK_POSITIONS).astype(jnp.int32)
            keys = lax.dynamic_index_in_dim(lax.dynamic_slice_in_dim(cache_keys, start, BLOCK_POSITIONS, 0), group, 1, False)
            values = lax.dynamic_index_in_dim(lax.dynamic_slice_in_dim(cache_values, start, BLOCK_POSITIONS, 0), group, 1, False)
            return carry, block_partial(query, keys, values, scale)

        unused, (maxima, totals, outs) = lax.scan(step, jnp.float32(0.0), chosen)
        top = jnp.maximum(jnp.max(maxima, axis=0), own_max)
        factors = jnp.exp(maxima - top[None, :])
        own_factor = jnp.exp(own_max - top)
        numer = jnp.sum(factors[:, :, None] * outs, axis=0) + own_factor[:, None] * own_out
        denom = jnp.sum(factors * totals, axis=0) + own_factor * own_total
        return (numer / denom[:, None]).astype(jnp.bfloat16)

    heads = lax.map(one_head, jnp.arange(QUERY_HEADS, dtype=jnp.int32))
    attended = jnp.transpose(heads, (1, 0, 2))
    flat = attended.reshape(NEW_POSITIONS, QUERY_HEADS * HEAD_SIZE)
    projected = jnp.dot(flat, out_weight, preferred_element_type=jnp.float32).astype(jnp.bfloat16)
    return attended, projected
```

```python
import functools

import jax
import jax.numpy as jnp
from jax import lax
from jax.experimental import pallas as pl
from jax.experimental.pallas import tpu as pltpu
from jax.sharding import PartitionSpec as P

Y, Z, X = 4, 8, 4
BLOCK_POSITIONS = 4096
MOST = 3
CHUNK = 1024
NEG = -1e30
MESH = pl.DeviceIdType.MESH
F32, BF16 = jnp.float32, jnp.bfloat16


def offsets(n):
    near = []
    for d in range(1, n // 2 + 1):
        near.append(d)
        if d != n - d:
            near.append(n - d)
    return near


ZOFF, YOFF = offsets(Z), offsets(Y)


def dot_t(a, b):
    return lax.dot_general(a, b, (((1,), (1,)), ((), ())), preferred_element_type=F32)


def dot(a, b):
    return jnp.dot(a, b, preferred_element_type=F32)


def place(y, z, c):
    return (lax.rem(y, Y) * Z + lax.rem(z, Z)) * 2 + lax.rem(c, 2)


class Gather:
    def __init__(self, buf, y, z, c, kv, zs, ys, cs, ss):
        self.buf, self.y, self.z, self.c, self.kv = buf, y, z, c, kv
        self.zs, self.ys, self.cs, self.ss = zs, ys, cs, ss

    def copy(self, index, sem, to):
        return pltpu.make_async_remote_copy(
            src_ref=self.buf.at[index], dst_ref=self.buf.at[index],
            send_sem=self.ss, recv_sem=sem, device_id=(to, self.kv), device_id_type=MESH)

    def spread(self, jz):
        y, z, c = self.y, self.z, self.c
        index = place(y, z + Z - ([0] + ZOFF)[jz], c)
        for jy, dy in enumerate(YOFF):
            self.copy(index, self.ys.at[jz, jy], place(y + dy, z, c)).start()
        self.copy(index, self.cs, place(y, z, c + 1)).start()

    def start(self):
        y, z, c = self.y, self.z, self.c
        index = place(y, z, c)
        for j, dz in enumerate(ZOFF):
            self.copy(index, self.zs.at[j], place(y, z + dz, c)).start()
        self.spread(0)

    def along_z(self, jz):
        y, z, c = self.y, self.z, self.c
        index = place(y, z + Z - ZOFF[jz - 1], c)
        self.copy(index, self.zs.at[jz - 1], place(y, z, c + 1)).wait_recv()
        self.spread(jz)

    def along_y(self, jz):
        y, z, c = self.y, self.z, self.c
        for jy, dy in enumerate(YOFF):
            index = place(y + Y - dy, z + Z - ([0] + ZOFF)[jz], c)
            self.copy(index, self.ys.at[jz, jy], place(y, z, c + 1)).wait_recv()
            self.copy(index, self.cs, place(y, z, c + 1)).start()

    def finish(self):
        other = place(self.y, self.z, self.c + 1)
        half = self.buf.at[pl.ds(0, Y * Z)]
        pltpu.make_async_remote_copy(src_ref=half, dst_ref=half, send_sem=self.ss, recv_sem=self.cs,
                                     device_id=(other, self.kv), device_id_type=MESH).wait_recv()

    def drain(self):
        other = place(self.y, self.z, self.c + 1)
        sent = self.buf.at[pl.ds(0, (Z - 1) + Z * (Y - 1) + Y * Z)]
        pltpu.make_async_remote_copy(src_ref=sent, dst_ref=sent, send_sem=self.ss, recv_sem=self.cs,
                                     device_id=(other, self.kv), device_id_type=MESH).wait_send()


def kernel(q_ref, sk_ref, sv_ref, gat_ref, kc_ref, vc_ref, w_ref, att_ref, proj_ref,
           kraw, vraw, k0, k1, v0, v1, wv, buf, buf2, f32s, kv32, d32, qaug, acc, mm, ll, ob, pf, pay, recv,
           own_o, own_l, xp, xr,
           loc, z1, y1, c1, s1, z2, y2, c2, s2, ar, asend, xs, xrs):
    n = Y * Z * 2
    me = lax.axis_index("ctx")
    kv = lax.axis_index("kvh")
    c = lax.rem(me, 2)
    z = lax.rem(lax.div(me, 2), Z)
    y = lax.div(me, 2 * Z)
    heads = gat_ref.shape[0]
    topk = gat_ref.shape[1]
    rows = q_ref.shape[0] // heads
    per = heads // 2
    width = q_ref.shape[1]
    bp = BLOCK_POSITIONS
    np_ = n * rows
    qr = rows * heads
    log2e = 1.4426950408889634
    c2s = width ** -0.5 * log2e

    kcopy = pltpu.make_async_copy(kc_ref, kraw, loc.at[0])
    vcopy = pltpu.make_async_copy(vc_ref, vraw, loc.at[1])
    wcopy = pltpu.make_async_copy(w_ref, wv, loc.at[2])
    kcopy.start()
    vcopy.start()
    wcopy.start()

    bar = pltpu.get_barrier_semaphore()

    def greet(i, _):
        pl.semaphore_signal(bar, inc=1, device_id=(lax.rem(me + i, n), kv), device_id_type=MESH)
        return 0

    lax.fori_loop(1, n, greet, 0)
    for dx in range(1, X):
        pl.semaphore_signal(bar, inc=1, device_id=(me, lax.rem(kv + dx, X)), device_id_type=MESH)
    buf[me, 0:qr, :] = q_ref[...]
    kvr = sk_ref.shape[0]
    buf[me, qr:qr + 2 * kvr, :] = jnp.concatenate([sk_ref[...], sv_ref[...]], axis=0)
    pl.semaphore_wait(bar, n - 1 + X - 1)

    g1 = Gather(buf, y, z, c, kv, z1, y1, c1, s1)
    g1.start()

    lane = lax.broadcasted_iota(jnp.int32, (heads, 2 * n), 1)
    block_of = lax.rem(lane, n) * 2 + lax.div(lane, n)
    gat = gat_ref[...]
    chosen = jnp.zeros((heads, 2 * n), jnp.int32)
    for t in range(topk):
        chosen = jnp.maximum(chosen, (gat[:, t:t + 1] == block_of).astype(jnp.int32))
    count = jnp.zeros((1, 2 * n), jnp.int32)
    hm = [jnp.full((1, 2 * n), -1, jnp.int32) for _ in range(MOST)]
    for h in range(heads):
        ch = chosen[h:h + 1, :]
        for s in range(MOST):
            hm[s] = jnp.where((ch == 1) & (count == s), h, hm[s])
        count = count + ch
    lane1 = lax.broadcasted_iota(jnp.int32, (1, 2 * n), 1)
    own_heads = [[jnp.maximum(jnp.max(jnp.where(lane1 == b * n + me, hm[s], -1)), 0) for s in range(MOST)]
                 for b in range(2)]

    def split(raw, even, odd, first, last):
        part = d32.shape[0]

        def step(i, _):
            d32[...] = raw[pl.ds(pl.multiple_of(i * part, part), part), :].astype(F32)
            to = pl.ds(pl.multiple_of(i * (part // 2), part // 2), part // 2)
            even[to, :] = d32[pl.ds(0, part // 2, stride=2), :].astype(BF16)
            odd[to, :] = d32[pl.ds(1, part // 2, stride=2), :].astype(BF16)
            return 0

        lax.fori_loop(first, last, step, 0)

    parts = kraw.shape[0] // d32.shape[0]
    kcopy.wait()
    nz = len(ZOFF)
    for j in range(1, nz + 1):
        split(kraw, k0, k1, (j - 1) * parts // nz, j * parts // nz)
        g1.along_z(j)
    vcopy.wait()
    for j in range(nz + 1):
        split(vraw, v0, v1, j * parts // (nz + 1), (j + 1) * parts // (nz + 1))
        g1.along_y(j)
    g1.finish()

    def widen(i, _):
        f32s[pl.ds(pl.multiple_of(i * qr, qr), qr), :] = buf[i, 0:qr, :].astype(F32)
        kv32[pl.ds(pl.multiple_of(i * 2 * kvr, 2 * kvr), 2 * kvr), :] = buf[i, qr:qr + 2 * kvr, :].astype(F32)
        return 0

    lax.fori_loop(0, n, widen, 0)

    for b in range(2):
        for s in range(MOST):
            h = own_heads[b][s]
            qh = f32s[pl.ds(h, np_, stride=heads), :]
            first = (h < per).astype(F32)
            at = pl.ds(s * np_, np_)
            qaug[b, at, :] = jnp.concatenate([qh * first, qh * (1.0 - first)], axis=1).astype(BF16)

    nb = bp // CHUNK
    for b in range(2):
        acc[...] = jnp.zeros_like(acc)
        ll[...] = jnp.zeros_like(ll)
        mm[...] = jnp.full_like(mm, NEG)

        def step(i, _):
            at = pl.ds(pl.multiple_of(b * bp + i * CHUNK, CHUNK), CHUNK)
            kc = jnp.concatenate([k0[at, :], k1[at, :]], axis=1)
            vc = jnp.concatenate([v0[at, :], v1[at, :]], axis=1)
            for s in range(MOST):
                sl = pl.ds(s * np_, np_)
                sc = dot_t(qaug[b, sl, :], kc)
                m0 = mm[sl, :]
                m1 = jnp.maximum(m0, jnp.max(sc, axis=1, keepdims=True) * c2s)
                p = jnp.exp2(sc * c2s - m1[:, :1])
                al = jnp.exp2(m0 - m1)
                ps = p[:, :128]
                for j in range(1, CHUNK // 128):
                    ps = ps + p[:, j * 128:(j + 1) * 128]
                ll[sl, :] = ll[sl, :] * al + ps
                mm[sl, :] = m1
                acc[sl, :] = acc[sl, :] * jnp.concatenate([al, al], axis=1) + dot(p.astype(BF16), vc)
            return 0

        lax.fori_loop(0, nb, step, 0)

        ln = lax.broadcasted_iota(jnp.int32, (np_, 128), 1)
        rw = lax.rem(lax.broadcasted_iota(jnp.int32, (np_, 128), 0), rows)
        stat = jnp.zeros((np_, 128), F32)
        for s in range(MOST):
            sl = pl.ds(s * np_, np_)
            tot = jnp.sum(ll[sl, :], axis=1, keepdims=True)
            lse = mm[sl, :] + jnp.log2(tot)
            first = own_heads[b][s] < per
            ob[s] = jnp.where(first, acc[sl, 0:128], acc[sl, 128:256]) * (1.0 / tot)
            hi = lse.astype(BF16).astype(F32)
            mid = (lse - hi).astype(BF16).astype(F32)
            lo = (lse - hi) - mid
            val = jnp.where(ln < 16, hi, jnp.where(ln < 32, mid, lo))
            stat = jnp.where((lax.rem(ln, 16) == s * rows + rw) & (ln < 48), val, stat)
        ob[MOST] = stat

        def pack(j, _):
            for s in range(MOST + 1):
                x = ob[s, pl.ds(pl.multiple_of(j * 8, 8), 8), :]
                pf[s * rows:(s + 1) * rows, :] = x[0:rows]
                pf[16 + s * rows:16 + (s + 1) * rows, :] = x[rows:2 * rows]
            pay[b, 2 * j] = pf[0:16, :].astype(BF16)
            pay[b, 2 * j + 1] = pf[16:32, :].astype(BF16)
            return 0

        lax.fori_loop(0, n // 2, pack, 0)
        recv[b, me] = pay[b, me]

        def send(i, _):
            to = lax.rem(me + i, n)
            pltpu.make_async_remote_copy(src_ref=pay.at[b, to], dst_ref=recv.at[b, me], send_sem=asend,
                                         recv_sem=ar.at[b], device_id=(to, kv), device_id_type=MESH).start()
            return 0

        lax.fori_loop(1, n, send, 0)

    kk, vvv = [], []
    for g in range(2):
        kk.append(jnp.concatenate([kv32[pl.ds(2 * i + g, n, stride=2 * kvr), :] for i in range(rows)], axis=0))
        vvv.append(jnp.concatenate([kv32[pl.ds(kvr + 2 * i + g, n, stride=2 * kvr), :] for i in range(rows)], axis=0))
    ks = jnp.concatenate(kk, axis=1).astype(BF16)
    vs = jnp.concatenate(vvv, axis=1).astype(BF16)
    qf = q_ref[...].astype(F32)
    rid = lax.broadcasted_iota(jnp.int32, (qr, 128), 0)
    first = (lax.rem(rid, heads) < per).astype(F32)
    qo = jnp.concatenate([qf * first, qf * (1.0 - first)], axis=1).astype(BF16)
    sc = dot_t(qo, ks) * c2s
    kid = lax.broadcasted_iota(jnp.int32, (qr, np_), 1)
    key_pos = lax.rem(kid, n) * rows + lax.div(kid, n)
    row_pos = me * rows + lax.div(lax.broadcasted_iota(jnp.int32, (qr, np_), 0), heads)
    seen = key_pos <= row_pos
    sc = jnp.where(seen, sc, NEG)
    om = jnp.max(sc, axis=1, keepdims=True)
    ow = jnp.where(seen, jnp.exp2(sc - om), 0.0)
    ot = jnp.sum(ow, axis=1, keepdims=True)
    oo = dot(ow.astype(BF16), vs)
    own_o[...] = jnp.where(first > 0.5, oo[:, 0:128], oo[:, 128:256]) * (1.0 / ot)
    own_l[...] = jnp.broadcast_to(om + jnp.log2(ot), (qr, 128))

    for b in range(2):
        rest = pay.at[b, pl.ds(0, n - 1)]
        pltpu.make_async_remote_copy(src_ref=rest, dst_ref=rest, send_sem=asend, recv_sem=ar.at[b],
                                     device_id=(lax.rem(me + 1, n), kv), device_id_type=MESH).wait_recv()
        f32s[b * n * 16:(b + 1) * n * 16, :] = recv[b].reshape(n * 16, 128).astype(F32)
    st = sum(f32s[pl.ds(MOST * rows + i, 2 * n, stride=16), :] for i in range(rows))
    st = (st + pltpu.roll(st, 128 - 16, 1)) + pltpu.roll(st, 128 - 32, 1)
    st = st.T
    hid = lax.broadcasted_iota(jnp.int32, (heads, 2 * n), 0)
    for i in range(rows):
        at = pl.ds(i * heads, heads)
        own = own_l[at, 0:1]
        top = own
        xs_ = []
        for s in range(MOST):
            x = jnp.where(hm[s] == hid, st[s * rows + i:s * rows + i + 1, :], NEG)
            xs_.append(x)
            top = jnp.maximum(top, jnp.max(x, axis=1, keepdims=True))
        share = jnp.exp2(own - top)
        den = share
        num = share * own_o[at, :]
        for s in range(MOST):
            wt = jnp.exp2(xs_[s] - top)
            den = den + jnp.sum(wt, axis=1, keepdims=True)
            hi = wt.astype(BF16)
            lo = (wt - hi.astype(F32)).astype(BF16)
            r = f32s[pl.ds(s * rows + i, 2 * n, stride=16), :].astype(BF16)
            both = dot(jnp.concatenate([hi, lo], axis=0), r)
            num = num + (both[0:heads] + both[heads:2 * heads])
        a = (num / den).astype(BF16)
        att_ref[at, :] = a
        buf2[me, at, :] = a

    g2 = Gather(buf2, y, z, c, kv, z2, y2, c2, s2)
    g2.start()
    for j in range(1, nz + 1):
        g2.along_z(j)
    for j in range(nz + 1):
        g2.along_y(j)
    g2.finish()

    def widen2(i, _):
        f32s[pl.ds(pl.multiple_of(i * qr, qr), qr), :] = buf2[i].astype(F32)
        return 0

    lax.fori_loop(0, n, widen2, 0)
    wcopy.wait()
    out = jnp.zeros((np_, 128), F32)
    for h in range(0, heads, 2):
        a = jnp.concatenate([f32s[pl.ds(h, np_, stride=heads), :], f32s[pl.ds(h + 1, np_, stride=heads), :]], axis=1)
        out = out + dot(a.astype(BF16), wv[h * width:(h + 2) * width, :])
    share = np_ // X
    for x in range(X):
        xp[x] = out[x * share:(x + 1) * share].astype(BF16)
    xr[kv] = xp[kv]
    for dx in range(1, X):
        to = lax.rem(kv + dx, X)
        pltpu.make_async_remote_copy(src_ref=xp.at[to], dst_ref=xr.at[kv], send_sem=xs.at[dx - 1],
                                     recv_sem=xrs.at[dx - 1], device_id=(me, to), device_id_type=MESH).start()
    for dx in range(1, X):
        to = lax.rem(kv + dx, X)
        pltpu.make_async_remote_copy(src_ref=xp.at[to], dst_ref=xr.at[lax.rem(kv + X - dx, X)], send_sem=xs.at[dx - 1],
                                     recv_sem=xrs.at[dx - 1], device_id=(me, to), device_id_type=MESH).wait()
    total = xr[0].astype(F32)
    for x in range(1, X):
        total = total + xr[x].astype(F32)
    proj_ref[...] = total.astype(BF16)

    g1.drain()
    g2.drain()
    for b in range(2):
        rest = pay.at[b, pl.ds(0, n - 1)]
        pltpu.make_async_remote_copy(src_ref=rest, dst_ref=rest, send_sem=asend, recv_sem=ar.at[b],
                                     device_id=(lax.rem(me + 1, n), kv), device_id_type=MESH).wait_send()


def local(queries, span_keys, span_values, cache_keys, cache_values, gating, out_weight):
    rows, heads, width = queries.shape
    groups = span_keys.shape[1]
    n = Y * Z * 2
    np_ = n * rows
    qr = rows * heads
    kvr = rows * groups
    bp = BLOCK_POSITIONS
    raw = 2 * bp * groups
    part = min(1024, raw)
    nzo, nyo = len(ZOFF), len(YOFF)
    vm = pltpu.VMEM
    dma = pltpu.SemaphoreType.DMA
    scratch = [
        vm((raw, width), BF16), vm((raw, width), BF16),
        vm((2 * bp, width), BF16), vm((2 * bp, width), BF16), vm((2 * bp, width), BF16), vm((2 * bp, width), BF16),
        vm(out_weight.shape, BF16),
        vm((n, qr + 2 * kvr, width), BF16), vm((n, qr, width), BF16),
        vm((n * qr, width), F32), vm((n * 2 * kvr, width), F32), vm((part, width), F32),
        vm((2, MOST * np_, 2 * width), BF16),
        vm((MOST * np_, 2 * width), F32), vm((MOST * np_, width), F32), vm((MOST * np_, width), F32),
        vm((MOST + 1, np_, width), F32), vm((32, width), F32),
        vm((2, n, 16, width), BF16), vm((2, n, 16, width), BF16),
        vm((qr, width), F32), vm((qr, width), F32),
        vm((X, np_ // X, width), BF16), vm((X, np_ // X, width), BF16),
        dma((3,)),
        dma((nzo,)), dma((nzo + 1, nyo)), dma, dma,
        dma((nzo,)), dma((nzo + 1, nyo)), dma, dma,
        dma((2,)), dma, dma((X - 1,)), dma((X - 1,)),
    ]
    inv = pl.BlockSpec(memory_space=pltpu.VMEM)
    anyw = pl.BlockSpec(memory_space=pl.ANY)
    att, proj = pl.pallas_call(
        kernel,
        out_shape=(jax.ShapeDtypeStruct((qr, width), BF16), jax.ShapeDtypeStruct((np_ // X, width), BF16)),
        in_specs=[inv, inv, inv, inv, anyw, anyw, anyw],
        out_specs=(inv, inv),
        scratch_shapes=scratch,
        compiler_params=pltpu.CompilerParams(collective_id=0, has_side_effects=True, vmem_limit_bytes=60 << 20),
        name="sparse_attention",
    )(
        queries.reshape(qr, width), span_keys.reshape(kvr, width), span_values.reshape(kvr, width), gating,
        cache_keys.reshape(raw, width), cache_values.reshape(raw, width), out_weight,
    )
    return att.reshape(rows, heads, width), proj


def solution(mesh):
    placed = (
        P("ctx", "kvh", None),
        P("ctx", "kvh", None),
        P("ctx", "kvh", None),
        P("ctx", "kvh", None),
        P("ctx", "kvh", None),
        P("kvh", None),
        P("kvh", "ctx"),
    )
    return jax.shard_map(
        local,
        mesh=mesh,
        in_specs=placed,
        out_specs=(P("ctx", "kvh", None), P("kvh", "ctx")),
        check_vma=False,
    )
```

```python
import functools

import jax
import jax.numpy as jnp
from jax import lax
from jax.experimental import pallas as pl
from jax.experimental.pallas import tpu as pltpu
from jax.sharding import PartitionSpec as P

Y, Z, X = 4, 8, 4
BLOCK_POSITIONS = 4096
MOST = 3
CHUNK = 1024
NEG = -1e30
MESH = pl.DeviceIdType.MESH
F32, BF16 = jnp.float32, jnp.bfloat16


def far_first(n):
    return sorted(range(n), key=lambda d: -min(d, n - d))


def near_first(n):
    return far_first(n)[:-1][::-1]


def dot_t(a, b):
    return lax.dot_general(a, b, (((1,), (1,)), ((), ())), preferred_element_type=F32)


def dot(a, b):
    return jnp.dot(a, b, preferred_element_type=F32)


class Comm:
    def __init__(self):
        self.me = lax.axis_index("ctx")
        self.kv = lax.axis_index("kvh")
        self.c = lax.rem(self.me, 2)
        self.z = lax.rem(lax.div(self.me, 2), Z)
        self.y = lax.div(self.me, 2 * Z)
        self.zc = 2 * self.z + self.c

    def rank(self, dy, dz, dc):
        return (lax.rem(self.y + dy, Y) * Z + lax.rem(self.z + dz, Z)) * 2 + lax.rem(self.c + dc, 2)

    def y_of(self, dy):
        return lax.rem(self.y + dy, Y)

    def zc_of(self, dz):
        return 2 * lax.rem(self.z + dz, Z) + self.c

    def copy(self, ref, send, recv, dy, dz, dc):
        return pltpu.make_async_remote_copy(src_ref=ref, dst_ref=ref, send_sem=send, recv_sem=recv,
                                            device_id=(self.rank(dy, dz, dc), self.kv), device_id_type=MESH)


class GatherZ:
    def __init__(self, m, buf, at, zs, ys, cs, sends):
        self.m, self.buf, self.at = m, buf, at
        self.zs, self.ys, self.cs, self.sends = zs, ys, cs, sends

    def spread(self, dz):
        m = self.m
        ref = self.buf.at[m.y, m.zc_of(Z - dz), self.at]
        for dy in far_first(Y)[:-1]:
            m.copy(ref, self.sends.at[1], self.ys.at[dz, dy - 1], dy, 0, 0).start()

    def start(self):
        m = self.m
        ref = self.buf.at[m.y, m.zc, self.at]
        for dz in far_first(Z)[:-1]:
            m.copy(ref, self.sends.at[0], self.zs.at[dz - 1], 0, dz, 0).start()
        self.spread(0)

    def along_z(self, dz):
        m = self.m
        m.copy(self.buf.at[m.y, m.zc_of(Z - dz), self.at], self.sends.at[0], self.zs.at[dz - 1], 0, dz, 0).wait_recv()
        self.spread(dz)

    def along_y(self, dz):
        m = self.m
        zc = m.zc_of(Z - dz)
        for dy in near_first(Y):
            m.copy(self.buf.at[m.y_of(Y - dy), zc, self.at], self.sends.at[1], self.ys.at[dz, dy - 1], dy, 0, 0).wait_recv()
        m.copy(self.buf.at[:, zc, self.at], self.sends.at[2], self.cs, 0, 0, 1).start()

    def finish(self):
        self.m.copy(self.buf.at[:, pl.ds(0, Z), self.at], self.sends.at[2], self.cs, 0, 0, 1).wait_recv()

    def drain(self):
        m = self.m
        m.copy(self.buf.at[0, pl.ds(0, Z - 1), self.at], self.sends.at[0], self.cs, 0, 0, 1).wait_send()
        m.copy(self.buf.at[pl.ds(0, Y - 1), pl.ds(0, Z), self.at], self.sends.at[1], self.cs, 0, 0, 1).wait_send()
        m.copy(self.buf.at[:, pl.ds(0, Z), self.at], self.sends.at[2], self.cs, 0, 0, 1).wait_send()


class GatherY:
    def __init__(self, m, buf, at, ys, zs, cs, sends):
        self.m, self.buf, self.at = m, buf, at
        self.ys, self.zs, self.cs, self.sends = ys, zs, cs, sends

    def start(self):
        m = self.m
        ref = self.buf.at[m.y, m.zc, self.at]
        for dy in far_first(Y)[:-1]:
            m.copy(ref, self.sends.at[0], self.ys.at[dy - 1], dy, 0, 0).start()

    def forward(self):
        m = self.m
        for dy in near_first(Y):
            m.copy(self.buf.at[m.y_of(Y - dy), m.zc, self.at], self.sends.at[0], self.ys.at[dy - 1], dy, 0, 0).wait_recv()
        ref = self.buf.at[:, m.zc, self.at]
        for dz in far_first(Z)[:-1]:
            m.copy(ref, self.sends.at[1], self.zs.at[dz - 1], 0, dz, 0).start()
        m.copy(ref, self.sends.at[2], self.cs, 0, 0, 1).start()

    def across(self, dz):
        m = self.m
        ref = self.buf.at[:, m.zc_of(Z - dz), self.at]
        m.copy(ref, self.sends.at[1], self.zs.at[dz - 1], 0, dz, 0).wait_recv()
        m.copy(ref, self.sends.at[2], self.cs, 0, 0, 1).start()

    def finish(self):
        self.m.copy(self.buf.at[:, pl.ds(0, Z), self.at], self.sends.at[2], self.cs, 0, 0, 1).wait_recv()

    def drain(self):
        m = self.m
        m.copy(self.buf.at[0, pl.ds(0, Y - 1), self.at], self.sends.at[0], self.cs, 0, 0, 1).wait_send()
        m.copy(self.buf.at[:, pl.ds(0, Z - 1), self.at], self.sends.at[1], self.cs, 0, 0, 1).wait_send()
        m.copy(self.buf.at[:, pl.ds(0, Z), self.at], self.sends.at[2], self.cs, 0, 0, 1).wait_send()


class Gather:
    def __init__(self, m, buf, sems):
        rows = buf.shape[2]
        cut = rows - rows // 4
        self.a = GatherZ(m, buf, pl.ds(0, cut), *sems[:4])
        self.b = GatherY(m, buf, pl.ds(cut, rows - cut), *sems[4:])

    def run(self, beside):
        a, b = self.a, self.b
        b.start()
        a.start()
        near = near_first(Z)
        for i, dz in enumerate(near):
            beside()
            a.along_z(dz)
            if i == min(1, len(near) - 1):
                b.forward()
        beside()
        a.along_y(0)
        for dz in near:
            beside()
            a.along_y(dz)
            b.across(dz)
        a.finish()
        b.finish()

    def drain(self):
        self.a.drain()
        self.b.drain()


def kernel(q_ref, sk_ref, sv_ref, gat_ref, kc_ref, vc_ref, w_ref, att_ref, part_ref,
           kraw, vraw, k0, k1, v0, v1, wv, buf, buf2, bufkv, f32s, kv32, d32, qaug,
           sb, cm, pb, alb, acc, mm, ll, ob, pf, pay, recv, own_o, own_l, xp,
           loc, ar, asend, xs, xrs, *sems):
    m = Comm()
    n = Y * Z * 2
    me, kv = m.me, m.kv
    heads, topk = gat_ref.shape
    rows = q_ref.shape[0] // heads
    per = heads // 2
    width = q_ref.shape[1]
    bp = BLOCK_POSITIONS
    np_ = n * rows
    qr = rows * heads
    kvr = sk_ref.shape[0]
    row = 2 * Z * rows
    hp = Y // 2 * row
    c2s = width ** -0.5 * 1.4426950408889634

    kcopy = pltpu.make_async_copy(kc_ref, kraw, loc.at[0])
    vcopy = pltpu.make_async_copy(vc_ref, vraw, loc.at[1])
    wcopy = pltpu.make_async_copy(w_ref, wv, loc.at[2])
    bar = pltpu.get_barrier_semaphore()
    for dz in far_first(Z)[:-1]:
        pl.semaphore_signal(bar, inc=1, device_id=(m.rank(0, dz, 0), kv), device_id_type=MESH)
    for dy in far_first(Y)[:-1]:
        pl.semaphore_signal(bar, inc=1, device_id=(m.rank(dy, 0, 0), kv), device_id_type=MESH)
    pl.semaphore_signal(bar, inc=1, device_id=(m.rank(0, 0, 1), kv), device_id_type=MESH)
    for dx in range(1, X):
        pl.semaphore_signal(bar, inc=1, device_id=(me, lax.rem(kv + dx, X)), device_id_type=MESH)
    kcopy.start()
    vcopy.start()
    wcopy.start()
    buf[m.y, m.zc] = q_ref[...]
    bufkv[m.y, m.zc] = jnp.concatenate([sk_ref[...], sv_ref[...]], axis=0)

    lane = lax.broadcasted_iota(jnp.int32, (heads, 2 * n), 1)
    block_of = lax.rem(lane, n) * 2 + lax.div(lane, n)
    gat = gat_ref[...]
    chosen = jnp.zeros((heads, 2 * n), jnp.int32)
    for t in range(topk):
        chosen = jnp.maximum(chosen, (gat[:, t:t + 1] == block_of).astype(jnp.int32))
    count = jnp.zeros((1, 2 * n), jnp.int32)
    hm = [jnp.full((1, 2 * n), -1, jnp.int32) for _ in range(MOST)]
    for h in range(heads):
        ch = chosen[h:h + 1, :]
        for s in range(MOST):
            hm[s] = jnp.where((ch == 1) & (count == s), h, hm[s])
        count = count + ch
    lane1 = lax.broadcasted_iota(jnp.int32, (1, 2 * n), 1)
    own_heads = [[jnp.maximum(jnp.max(jnp.where(lane1 == b * n + me, hm[s], -1)), 0) for s in range(MOST)]
                 for b in range(2)]

    part = d32.shape[0]
    parts = kraw.shape[0] // part

    def split(raw, even, odd, i):
        at = pl.ds(i * part, part)
        to = pl.ds(i * (part // 2), part // 2)
        d32[...] = raw[at, :].astype(F32)
        even[to, :] = d32[pl.ds(0, part // 2, stride=2), :].astype(BF16)
        odd[to, :] = d32[pl.ds(1, part // 2, stride=2), :].astype(BF16)

    def pieces():
        kcopy.wait()
        for i in range(parts):
            split(kraw, k0, k1, i)
            yield
        vcopy.wait()
        for i in range(parts):
            split(vraw, v0, v1, i)
            yield

    work = pieces()
    todo = 2 * parts
    each = -(-todo // (2 * Z + 1))

    def beside():
        for _ in range(each):
            next(work, None)

    beside()
    pl.semaphore_wait(bar, Z - 1 + Y - 1 + 1 + X - 1)
    g1 = Gather(m, buf, sems[0:8])
    g1.run(beside)
    for _ in work:
        pass
    g3 = GatherZ(m, bufkv, pl.ds(0, 2 * kvr), *sems[16:20])
    g3.start()

    def widen(i, _):
        zc = lax.rem(i, 2 * Z)
        f32s[pl.ds(pl.multiple_of(i * qr, qr), qr), :] = buf[lax.div(i, 2 * Z), zc].astype(F32)
        return 0

    lax.fori_loop(0, n, widen, 0)

    nb = bp // CHUNK
    far = far_first(Y)
    for half in range(2):
        dys = far[half * (Y // 2):(half + 1) * (Y // 2)]
        for b in range(2):
            for s in range(MOST):
                h = own_heads[b][s]
                first = (h < per).astype(F32)
                for t, dy in enumerate(dys):
                    qh = f32s[pl.ds(m.y_of(dy) * (row * heads) + h, row, stride=heads), :]
                    qaug[b, s * hp + t * row:s * hp + (t + 1) * row, :] = jnp.concatenate(
                        [qh * first, qh * (1.0 - first)], axis=1).astype(BF16)

        def unit(b, _):
            def both(even, odd, i):
                at = pl.ds(pl.multiple_of(b * bp + i * CHUNK, CHUNK), CHUNK)
                return jnp.concatenate([even[at, :], odd[at, :]], axis=1)

            def score(slot, i):
                s = dot_t(qaug[b], both(k0, k1, i))
                sb[slot] = s
                top = s[:, :128]
                for j in range(1, CHUNK // 128):
                    top = jnp.maximum(top, s[:, j * 128:(j + 1) * 128])
                cm[slot] = top

            def soften(slot):
                m0 = mm[...]
                m1 = jnp.maximum(m0, jnp.max(cm[slot], axis=1, keepdims=True) * c2s)
                p = jnp.exp2(sb[slot] * c2s - m1[:, :1])
                al = jnp.exp2(m0 - m1)
                ps = p[:, :128]
                for j in range(1, CHUNK // 128):
                    ps = ps + p[:, j * 128:(j + 1) * 128]
                ll[...] = ll[...] * al + ps
                mm[...] = m1
                alb[slot] = al
                pb[slot] = p.astype(BF16)

            def gain(slot, i):
                al = alb[slot]
                acc[...] = acc[...] * jnp.concatenate([al, al], axis=1) + dot(pb[slot], both(v0, v1, i))

            acc[...] = jnp.zeros_like(acc)
            ll[...] = jnp.zeros_like(ll)
            mm[...] = jnp.full_like(mm, NEG)
            score(0, 0)
            score(1, 1)
            soften(0)
            for i in range(1, nb - 1):
                score((i + 1) % 2, i + 1)
                gain((i - 1) % 2, i - 1)
                soften(i % 2)
            gain(nb % 2, nb - 2)
            soften((nb - 1) % 2)
            gain((nb - 1) % 2, nb - 1)

            ln = lax.broadcasted_iota(jnp.int32, (hp, 128), 1)
            rw = lax.rem(lax.broadcasted_iota(jnp.int32, (hp, 128), 0), rows)
            stat = jnp.zeros((hp, 128), F32)
            for s in range(MOST):
                sl = pl.ds(s * hp, hp)
                tot = jnp.sum(ll[sl, :], axis=1, keepdims=True)
                lse = mm[sl, :] + jnp.log2(tot)
                first = jnp.where(b == 0, own_heads[0][s], own_heads[1][s]) < per
                ob[s] = jnp.where(first, acc[sl, 0:128], acc[sl, 128:256]) * (1.0 / tot)
                hi = lse.astype(BF16).astype(F32)
                mid = (lse - hi).astype(BF16).astype(F32)
                lo = (lse - hi) - mid
                val = jnp.where(ln < 16, hi, jnp.where(ln < 32, mid, lo))
                stat = jnp.where((lax.rem(ln, 16) == s * rows + rw) & (ln < 48), val, stat)
            ob[MOST] = stat
            for t, dy in enumerate(dys):
                to_y = m.y_of(dy) * (2 * Z)

                def pack(j, _):
                    for s in range(MOST + 1):
                        x = ob[s, pl.ds(pl.multiple_of(t * row + j * 8, 8), 8), :]
                        pf[s * rows:(s + 1) * rows, :] = x[0:rows]
                        pf[16 + s * rows:16 + (s + 1) * rows, :] = x[rows:2 * rows]
                    pay[b, to_y + 2 * j] = pf[0:16, :].astype(BF16)
                    pay[b, to_y + 2 * j + 1] = pf[16:32, :].astype(BF16)
                    return 0

                lax.fori_loop(0, Z, pack, 0)
            if 0 in dys:
                recv[b, me] = pay[b, me]

            def send(dy, dz, dc):
                to = m.rank(dy, dz, dc)
                pltpu.make_async_remote_copy(src_ref=pay.at[b, to], dst_ref=recv.at[b, me], send_sem=asend,
                                             recv_sem=ar.at[b], device_id=(to, kv), device_id_type=MESH).start()

            def sends(i, _):
                k = lax.div(i + 1, 2)
                dz = Z // 2 + jnp.where(lax.rem(i, 2) == 1, -k, k)
                for dy in dys:
                    for dc in range(2):
                        send(dy, dz, dc)
                return 0

            lax.fori_loop(0, Z - 1, sends, 0)
            for dy in dys:
                for dc in range(2):
                    if (dy, dc) != (0, 0):
                        send(dy, 0, dc)
            return 0

        lax.fori_loop(0, 2, unit, 0)
        if half == 0:
            for dz in near_first(Z):
                g3.along_z(dz)
    for dz in range(Z):
        g3.along_y(dz)
    g3.finish()

    def widenkv(i, _):
        zc = lax.rem(i, 2 * Z)
        kv32[pl.ds(pl.multiple_of(i * 2 * kvr, 2 * kvr), 2 * kvr), :] = bufkv[lax.div(i, 2 * Z), zc].astype(F32)
        return 0

    lax.fori_loop(0, n, widenkv, 0)
    kk, vvv = [], []
    for g in range(2):
        kk.append(jnp.concatenate([kv32[pl.ds(2 * i + g, n, stride=2 * kvr), :] for i in range(rows)], axis=0))
        vvv.append(jnp.concatenate([kv32[pl.ds(kvr + 2 * i + g, n, stride=2 * kvr), :] for i in range(rows)], axis=0))
    ks = jnp.concatenate(kk, axis=1).astype(BF16)
    vs = jnp.concatenate(vvv, axis=1).astype(BF16)
    qf = q_ref[...].astype(F32)
    rid = lax.broadcasted_iota(jnp.int32, (qr, 128), 0)
    first = (lax.rem(rid, heads) < per).astype(F32)
    qo = jnp.concatenate([qf * first, qf * (1.0 - first)], axis=1).astype(BF16)
    sc = dot_t(qo, ks) * c2s
    kid = lax.broadcasted_iota(jnp.int32, (qr, np_), 1)
    key_pos = lax.rem(kid, n) * rows + lax.div(kid, n)
    row_pos = me * rows + lax.div(lax.broadcasted_iota(jnp.int32, (qr, np_), 0), heads)
    seen = key_pos <= row_pos
    sc = jnp.where(seen, sc, NEG)
    om = jnp.max(sc, axis=1, keepdims=True)
    ow = jnp.where(seen, jnp.exp2(sc - om), 0.0)
    ot = jnp.sum(ow, axis=1, keepdims=True)
    oo = dot(ow.astype(BF16), vs)
    own_o[...] = jnp.where(first > 0.5, oo[:, 0:128], oo[:, 128:256]) * (1.0 / ot)
    own_l[...] = jnp.broadcast_to(om + jnp.log2(ot), (qr, 128))

    for b in range(2):
        rest = pay.at[b, pl.ds(0, n - 1)]
        pltpu.make_async_remote_copy(src_ref=rest, dst_ref=rest, send_sem=asend, recv_sem=ar.at[b],
                                     device_id=(m.rank(0, 1, 0), kv), device_id_type=MESH).wait_recv()
        f32s[b * n * 16:(b + 1) * n * 16, :] = recv[b].reshape(n * 16, 128).astype(F32)
    st = sum(f32s[pl.ds(MOST * rows + i, 2 * n, stride=16), :] for i in range(rows))
    st = (st + pltpu.roll(st, 128 - 16, 1)) + pltpu.roll(st, 128 - 32, 1)
    st = st.T
    hid = lax.broadcasted_iota(jnp.int32, (heads, 2 * n), 0)
    for i in range(rows):
        at = pl.ds(i * heads, heads)
        own = own_l[at, 0:1]
        top = own
        xs_ = []
        for s in range(MOST):
            x = jnp.where(hm[s] == hid, st[s * rows + i:s * rows + i + 1, :], NEG)
            xs_.append(x)
            top = jnp.maximum(top, jnp.max(x, axis=1, keepdims=True))
        share = jnp.exp2(own - top)
        den = share
        num = share * own_o[at, :]
        for s in range(MOST):
            wt = jnp.exp2(xs_[s] - top)
            den = den + jnp.sum(wt, axis=1, keepdims=True)
            hi = wt.astype(BF16)
            lo = (wt - hi.astype(F32)).astype(BF16)
            r = f32s[pl.ds(s * rows + i, 2 * n, stride=16), :].astype(BF16)
            two = dot(jnp.concatenate([hi, lo], axis=0), r)
            num = num + (two[0:heads] + two[heads:2 * heads])
        a = (num / den).astype(BF16)
        att_ref[at, :] = a
        buf2[m.y, m.zc, at, :] = a

    g2 = Gather(m, buf2, sems[8:16])
    g2.run(lambda: None)
    wcopy.wait()
    share = np_ // X
    per_x = n // X
    for dxs in (far_first(X)[:X // 2], far_first(X)[X // 2:]):
        for t, dx in enumerate(dxs):
            x = lax.rem(kv + dx, X)

            def widen2(i, _):
                j = x * per_x + i
                to = pl.ds(pl.multiple_of((t * per_x + i) * qr, qr), qr)
                f32s[to, :] = buf2[lax.div(j, 2 * Z), lax.rem(j, 2 * Z)].astype(F32)
                return 0

            lax.fori_loop(0, per_x, widen2, 0)
        out = jnp.zeros((len(dxs) * share, 128), F32)
        for h in range(0, heads, 2):
            a = jnp.concatenate([f32s[pl.ds(h + e, len(dxs) * share, stride=heads), :] for e in range(2)], axis=1)
            out = out + dot(a.astype(BF16), wv[h * width:(h + 2) * width, :])
        for t, dx in enumerate(dxs):
            x = lax.rem(kv + dx, X)
            piece = out[t * share:(t + 1) * share].astype(BF16)
            if dx == 0:
                part_ref[kv] = piece
            else:
                xp[dx - 1] = piece
                pltpu.make_async_remote_copy(src_ref=xp.at[dx - 1], dst_ref=part_ref.at[kv], send_sem=xs.at[dx - 1],
                                             recv_sem=xrs.at[dx - 1], device_id=(me, x), device_id_type=MESH).start()
    g1.drain()
    g2.drain()
    g3.drain()
    for b in range(2):
        rest = pay.at[b, pl.ds(0, n - 1)]
        pltpu.make_async_remote_copy(src_ref=rest, dst_ref=rest, send_sem=asend, recv_sem=ar.at[b],
                                     device_id=(m.rank(0, 1, 0), kv), device_id_type=MESH).wait_send()
    for dx in range(1, X):
        pltpu.make_async_remote_copy(src_ref=xp.at[dx - 1], dst_ref=part_ref.at[lax.rem(kv + X - dx, X)],
                                     send_sem=xs.at[dx - 1], recv_sem=xrs.at[dx - 1],
                                     device_id=(me, lax.rem(kv + dx, X)), device_id_type=MESH).wait()


def close(att_ref, part_ref, a_ref, p_ref):
    a_ref[...] = att_ref[...]
    total = part_ref[0].astype(F32)
    for x in range(1, X):
        total = total + part_ref[x].astype(F32)
    p_ref[...] = total.astype(BF16)


def local(queries, span_keys, span_values, cache_keys, cache_values, gating, out_weight):
    rows, heads, width = queries.shape
    groups = span_keys.shape[1]
    n = Y * Z * 2
    np_ = n * rows
    qr = rows * heads
    kvr = rows * groups
    bp = BLOCK_POSITIONS
    raw = 2 * bp * groups
    part = min(1024, raw)
    unit = MOST * np_ // 2
    vm = pltpu.VMEM
    dma = pltpu.SemaphoreType.DMA
    along = [dma((Z - 1,)), dma((Z, Y - 1)), dma, dma((3,))]
    both = along + [dma((Y - 1,)), dma((Z - 1,)), dma, dma((3,))]
    scratch = [
        vm((raw, width), BF16), vm((raw, width), BF16),
        vm((2 * bp, width), BF16), vm((2 * bp, width), BF16), vm((2 * bp, width), BF16), vm((2 * bp, width), BF16),
        vm(out_weight.shape, BF16),
        vm((Y, 2 * Z, qr, width), BF16), vm((Y, 2 * Z, qr, width), BF16), vm((Y, 2 * Z, 2 * kvr, width), BF16),
        vm((n * qr, width), F32), vm((n * 2 * kvr, width), F32), vm((part, width), F32),
        vm((2, unit, 2 * width), BF16),
        vm((2, unit, CHUNK), F32), vm((2, unit, width), F32), vm((2, unit, CHUNK), BF16), vm((2, unit, width), F32),
        vm((unit, 2 * width), F32), vm((unit, width), F32), vm((unit, width), F32),
        vm((MOST + 1, np_ // 2, width), F32), vm((32, width), F32),
        vm((2, n, 16, width), BF16), vm((2, n, 16, width), BF16),
        vm((qr, width), F32), vm((qr, width), F32),
        vm((X - 1, np_ // X, width), BF16),
        dma((3,)), dma((2,)), dma, dma((X - 1,)), dma((X - 1,)),
        *both, *both, *along,
    ]
    inv = pl.BlockSpec(memory_space=pltpu.VMEM)
    anyw = pl.BlockSpec(memory_space=pl.ANY)
    att, parts = pl.pallas_call(
        kernel,
        out_shape=(jax.ShapeDtypeStruct((qr, width), BF16), jax.ShapeDtypeStruct((X, np_ // X, width), BF16)),
        in_specs=[inv, inv, inv, inv, anyw, anyw, anyw],
        out_specs=(inv, inv),
        scratch_shapes=scratch,
        compiler_params=pltpu.CompilerParams(collective_id=0, has_side_effects=True, vmem_limit_bytes=60 << 20),
        name="sparse_attention",
    )(
        queries.reshape(qr, width), span_keys.reshape(kvr, width), span_values.reshape(kvr, width), gating,
        cache_keys.reshape(raw, width), cache_values.reshape(raw, width), out_weight,
    )
    att, proj = pl.pallas_call(
        close,
        out_shape=(jax.ShapeDtypeStruct((qr, width), BF16), jax.ShapeDtypeStruct((np_ // X, width), BF16)),
        in_specs=[inv, inv],
        out_specs=(inv, inv),
        name="close",
    )(att, parts)
    return att.reshape(rows, heads, width), proj


def solution(mesh):
    placed = (
        P("ctx", "kvh", None),
        P("ctx", "kvh", None),
        P("ctx", "kvh", None),
        P("ctx", "kvh", None),
        P("ctx", "kvh", None),
        P("kvh", None),
        P("kvh", "ctx"),
    )
    return jax.shard_map(
        local,
        mesh=mesh,
        in_specs=placed,
        out_specs=(P("ctx", "kvh", None), P("kvh", "ctx")),
        check_vma=False,
    )
```

```python
import functools

import jax
import jax.numpy as jnp
from jax import lax
from jax.experimental import pallas as pl
from jax.experimental.pallas import tpu as pltpu
from jax.sharding import PartitionSpec as P

Y, Z, X = 4, 8, 4
BLOCK_POSITIONS = 4096
MOST = 3
CHUNK = 1024
NEG = -1e30
MESH = pl.DeviceIdType.MESH
F32, BF16 = jnp.float32, jnp.bfloat16


def far_first(n):
    return sorted(range(n), key=lambda d: -min(d, n - d))


def near_first(n):
    return far_first(n)[:-1][::-1]


def dot_t(a, b):
    return lax.dot_general(a, b, (((1,), (1,)), ((), ())), preferred_element_type=F32)


def dot(a, b):
    return jnp.dot(a, b, preferred_element_type=F32)


class Comm:
    def __init__(self):
        self.me = lax.axis_index("ctx")
        self.kv = lax.axis_index("kvh")
        self.c = lax.rem(self.me, 2)
        self.z = lax.rem(lax.div(self.me, 2), Z)
        self.y = lax.div(self.me, 2 * Z)

    def rank(self, dy, dz, dc):
        return (lax.rem(self.y + dy, Y) * Z + lax.rem(self.z + dz, Z)) * 2 + lax.rem(self.c + dc, 2)

    def y_of(self, dy):
        return lax.rem(self.y + dy, Y)

    def copy(self, ref, send, recv, dy, dz, dc):
        return pltpu.make_async_remote_copy(src_ref=ref, dst_ref=ref, send_sem=send, recv_sem=recv,
                                            device_id=(self.rank(dy, dz, dc), self.kv), device_id_type=MESH)


class GatherZ:
    def __init__(self, m, buf, at, slot, zs, ys, sends, ahead=()):
        self.m, self.buf, self.at, self.slot = m, buf, at, slot
        self.zs, self.ys, self.sends = zs, ys, sends
        self.ahead = ahead or far_first(Y)[:-1]

    def ref(self, dy, dz):
        return self.buf.at[self.m.y_of(dy), self.slot(dz), self.at]

    def spread(self, dz):
        m = self.m
        for dy in self.ahead:
            m.copy(self.ref(0, Z - dz), self.sends.at[1], self.ys.at[dz, dy - 1], dy, 0, 0).start()

    def start(self):
        m = self.m
        for dz in near_first(Z):
            m.copy(self.ref(0, 0), self.sends.at[0], self.zs.at[dz - 1], 0, dz, 0).start()
        self.spread(0)

    def along_z(self, dz):
        self.m.copy(self.ref(0, Z - dz), self.sends.at[0], self.zs.at[dz - 1], 0, dz, 0).wait_recv()
        self.spread(dz)

    def along_y(self, dy, dz):
        self.m.copy(self.ref(dy, Z - dz), self.sends.at[1], self.ys.at[dz, Y - dy - 1], Y - dy, 0, 0).wait_recv()

    def core(self, dy, dz, sem):
        self.m.copy(self.ref(dy, Z - dz), self.sends.at[2], sem, 0, 0, 1).start()

    def core_wait(self, number, sem):
        shards = self.buf.at[pl.ds(0, number // Z), pl.ds(0, Z), self.at]
        self.m.copy(shards, self.sends.at[2], sem, 0, 0, 1).wait_recv()

    def drain(self, core):
        m = self.m
        parts = [self.buf.at[0, pl.ds(0, Z - 1), self.at], self.buf.at[pl.ds(0, Y - 1), pl.ds(0, Z), self.at]]
        if core:
            parts.append(self.buf.at[:, pl.ds(0, Z), self.at])
        for i, part in enumerate(parts):
            m.copy(part, self.sends.at[i], self.zs.at[0], 0, 0, 1).wait_send()


class GatherY:
    def __init__(self, m, buf, at, slot, ys, zs, sends):
        self.m, self.buf, self.at, self.slot = m, buf, at, slot
        self.ys, self.zs, self.sends = ys, zs, sends

    def start(self):
        m = self.m
        ref = self.buf.at[m.y, self.slot(0), self.at]
        for dy in far_first(Y)[:-1]:
            m.copy(ref, self.sends.at[0], self.ys.at[dy - 1], dy, 0, 0).start()

    def forward(self):
        m = self.m
        for dy in near_first(Y):
            ref = self.buf.at[m.y_of(Y - dy), self.slot(0), self.at]
            m.copy(ref, self.sends.at[0], self.ys.at[dy - 1], dy, 0, 0).wait_recv()
        for dz in far_first(Z)[:-1]:
            m.copy(self.buf.at[:, self.slot(0), self.at], self.sends.at[1], self.zs.at[dz - 1], 0, dz, 0).start()

    def across(self, dz):
        ref = self.buf.at[:, self.slot(Z - dz), self.at]
        self.m.copy(ref, self.sends.at[1], self.zs.at[dz - 1], 0, dz, 0).wait_recv()

    def drain(self):
        m = self.m
        m.copy(self.buf.at[0, pl.ds(0, Y - 1), self.at], self.sends.at[0], self.zs.at[0], 0, 0, 1).wait_send()
        m.copy(self.buf.at[:, pl.ds(0, Z - 1), self.at], self.sends.at[1], self.zs.at[0], 0, 0, 1).wait_send()


def kernel(q_ref, sk_ref, sv_ref, gat_ref, kc_ref, vc_ref, w_ref, att_ref, part_ref,
           kraw, vraw, k0, k1, v0, v1, wv, buf, buf2, bufkv, f32s, kv32, d32, qaug,
           sb, cm, pb, alb, acc, mm, ll, ob, pf, pay, recv, own_o, own_l, xp,
           loc, ar, asend, xs, xrs, ws, wrs, c1, c3, *sems):
    m = Comm()
    zc = 2 * m.z + m.c

    def both_cores(dz):
        return 2 * lax.rem(m.z + dz, Z) + m.c

    def one_core(dz):
        return lax.rem(m.z + dz, Z)

    n = Y * Z * 2
    me, kv = m.me, m.kv
    heads, topk = gat_ref.shape
    rows = q_ref.shape[0] // heads
    per = heads // 2
    width = q_ref.shape[1]
    bp = BLOCK_POSITIONS
    np_ = n * rows
    qr = rows * heads
    kvr = sk_ref.shape[0]
    row = 2 * Z * rows
    hp = Y // 2 * row
    c2s = width ** -0.5 * 1.4426950408889634

    kcopy = pltpu.make_async_copy(kc_ref, kraw, loc.at[0])
    vcopy = pltpu.make_async_copy(vc_ref, vraw, loc.at[1])
    wcopy = pltpu.make_async_copy(w_ref, wv.at[m.c], loc.at[2])
    wgive = pltpu.make_async_remote_copy(src_ref=w_ref, dst_ref=wv.at[m.c], send_sem=ws, recv_sem=wrs,
                                         device_id=(m.rank(0, 0, 1), kv), device_id_type=MESH)
    bar = pltpu.get_barrier_semaphore()
    for dz in far_first(Z)[:-1]:
        pl.semaphore_signal(bar, inc=1, device_id=(m.rank(0, dz, 0), kv), device_id_type=MESH)
    for dy in far_first(Y)[:-1]:
        pl.semaphore_signal(bar, inc=1, device_id=(m.rank(dy, 0, 0), kv), device_id_type=MESH)
    for dx in range(X):
        for dc in range(2):
            if (dx, dc) != (0, 0):
                pl.semaphore_signal(bar, inc=1, device_id=(m.rank(0, 0, dc), lax.rem(kv + dx, X)), device_id_type=MESH)
    kcopy.start()
    vcopy.start()
    wcopy.start()
    buf[m.y, zc] = q_ref[...]
    bufkv[m.y, zc] = jnp.concatenate([sk_ref[...], sv_ref[...]], axis=0)

    lane = lax.broadcasted_iota(jnp.int32, (heads, 2 * n), 1)
    block_of = lax.rem(lane, n) * 2 + lax.div(lane, n)
    gat = gat_ref[...]
    chosen = jnp.zeros((heads, 2 * n), jnp.int32)
    for t in range(topk):
        chosen = jnp.maximum(chosen, (gat[:, t:t + 1] == block_of).astype(jnp.int32))
    count = jnp.zeros((1, 2 * n), jnp.int32)
    hm = [jnp.full((1, 2 * n), -1, jnp.int32) for _ in range(MOST)]
    for h in range(heads):
        ch = chosen[h:h + 1, :]
        for s in range(MOST):
            hm[s] = jnp.where((ch == 1) & (count == s), h, hm[s])
        count = count + ch
    lane1 = lax.broadcasted_iota(jnp.int32, (1, 2 * n), 1)
    own_heads = [[jnp.maximum(jnp.max(jnp.where(lane1 == b * n + me, hm[s], -1)), 0) for s in range(MOST)]
                 for b in range(2)]

    part = d32.shape[0]
    parts = kraw.shape[0] // part

    def split(raw, even, odd, i):
        at = pl.ds(i * part, part)
        to = pl.ds(i * (part // 2), part // 2)
        d32[...] = raw[at, :].astype(F32)
        even[to, :] = d32[pl.ds(0, part // 2, stride=2), :].astype(BF16)
        odd[to, :] = d32[pl.ds(1, part // 2, stride=2), :].astype(BF16)

    def pieces():
        kcopy.wait()
        for i in range(parts):
            split(kraw, k0, k1, i)
            yield
        vcopy.wait()
        for i in range(parts):
            split(vraw, v0, v1, i)
            yield

    work = pieces()
    todo = 2 * parts
    each = -(-todo // (2 * Z))

    def beside():
        for _ in range(each):
            next(work, None)

    beside()
    pl.semaphore_wait(bar, Z - 1 + Y - 1 + 2 * X - 1)

    near = near_first(Z)
    g1 = GatherZ(m, buf, pl.ds(0, qr), both_cores, sems[0], sems[1], sems[2], ahead=range(Y - 1, 0, -1))
    g1.start()
    g1.core(0, 0, c1.at[0])
    for dz in near:
        beside()
        g1.along_z(dz)
        g1.core(0, dz, c1.at[0])
    first_half = list(range(1, Y // 2))
    second_half = list(range(Y // 2, Y))
    for dz in [0] + near:
        beside()
        for dy in first_half:
            g1.along_y(dy, dz)
            g1.core(dy, dz, c1.at[0])
    for _ in work:
        pass
    g1.core_wait(Y * Z // 2, c1.at[0])
    wgive.start()
    g3 = GatherZ(m, bufkv, pl.ds(0, 2 * kvr), both_cores, sems[3], sems[4], sems[5])
    g3.start()

    nb = bp // CHUNK
    for half in range(2):
        dys = list(range(half * (Y // 2), (half + 1) * (Y // 2)))
        if half == 1:
            g1.core_wait(Y * Z // 2, c1.at[1])
        for dy in dys:
            yy = m.y_of(dy)

            def widen(i, _):
                f32s[pl.ds(pl.multiple_of((yy * (2 * Z) + i) * qr, qr), qr), :] = buf[yy, i].astype(F32)
                return 0

            lax.fori_loop(0, 2 * Z, widen, 0)
        for b in range(2):
            for s in range(MOST):
                h = own_heads[b][s]
                first = (h < per).astype(F32)
                for t, dy in enumerate(dys):
                    qh = f32s[pl.ds(m.y_of(dy) * (row * heads) + h, row, stride=heads), :]
                    qaug[b, s * hp + t * row:s * hp + (t + 1) * row, :] = jnp.concatenate(
                        [qh * first, qh * (1.0 - first)], axis=1).astype(BF16)

        def unit(b, _):
            def both(even, odd, i):
                at = pl.ds(pl.multiple_of(b * bp + i * CHUNK, CHUNK), CHUNK)
                return jnp.concatenate([even[at, :], odd[at, :]], axis=1)

            def score(slot, i):
                s = dot_t(qaug[b], both(k0, k1, i))
                sb[slot] = s
                top = s[:, :128]
                for j in range(1, CHUNK // 128):
                    top = jnp.maximum(top, s[:, j * 128:(j + 1) * 128])
                cm[slot] = top

            def soften(slot):
                m0 = mm[...]
                m1 = jnp.maximum(m0, jnp.max(cm[slot], axis=1, keepdims=True) * c2s)
                p = jnp.exp2(sb[slot] * c2s - m1[:, :1])
                al = jnp.exp2(m0 - m1)
                ps = p[:, :128]
                for j in range(1, CHUNK // 128):
                    ps = ps + p[:, j * 128:(j + 1) * 128]
                ll[...] = ll[...] * al + ps
                mm[...] = m1
                alb[slot] = al
                pb[slot] = p.astype(BF16)

            def gain(slot, i):
                al = alb[slot]
                acc[...] = acc[...] * jnp.concatenate([al, al], axis=1) + dot(pb[slot], both(v0, v1, i))

            acc[...] = jnp.zeros_like(acc)
            ll[...] = jnp.zeros_like(ll)
            mm[...] = jnp.full_like(mm, NEG)
            score(0, 0)
            score(1, 1)
            soften(0)
            for i in range(1, nb - 1):
                score((i + 1) % 2, i + 1)
                gain((i - 1) % 2, i - 1)
                soften(i % 2)
            gain(nb % 2, nb - 2)
            soften((nb - 1) % 2)
            gain((nb - 1) % 2, nb - 1)

            ln = lax.broadcasted_iota(jnp.int32, (hp, 128), 1)
            rw = lax.rem(lax.broadcasted_iota(jnp.int32, (hp, 128), 0), rows)
            stat = jnp.zeros((hp, 128), F32)
            for s in range(MOST):
                sl = pl.ds(s * hp, hp)
                tot = jnp.sum(ll[sl, :], axis=1, keepdims=True)
                lse = mm[sl, :] + jnp.log2(tot)
                first = jnp.where(b == 0, own_heads[0][s], own_heads[1][s]) < per
                ob[s] = jnp.where(first, acc[sl, 0:128], acc[sl, 128:256]) * (1.0 / tot)
                hi = lse.astype(BF16).astype(F32)
                mid = (lse - hi).astype(BF16).astype(F32)
                lo = (lse - hi) - mid
                val = jnp.where(ln < 16, hi, jnp.where(ln < 32, mid, lo))
                stat = jnp.where((lax.rem(ln, 16) == s * rows + rw) & (ln < 48), val, stat)
            ob[MOST] = stat
            for t, dy in enumerate(dys):
                for j in range(Z):
                    d = t * 2 * Z + 2 * j
                    for s in range(MOST + 1):
                        x = ob[s, d * rows:(d + 2) * rows, :]
                        pf[d * 16 + s * rows:d * 16 + (s + 1) * rows, :] = x[0:rows]
                        pf[(d + 1) * 16 + s * rows:(d + 1) * 16 + (s + 1) * rows, :] = x[rows:2 * rows]
                of_y = pf[t * 2 * Z * 16:(t + 1) * 2 * Z * 16, :].astype(BF16).reshape(2 * Z, 16, 128)
                pay[b, pl.ds(m.y_of(dy) * (2 * Z), 2 * Z)] = of_y
            if 0 in dys:
                recv[b, me] = pay[b, me]

            def send(dy, dz, dc):
                to = m.rank(dy, dz, dc)
                pltpu.make_async_remote_copy(src_ref=pay.at[b, to], dst_ref=recv.at[b, me], send_sem=asend,
                                             recv_sem=ar.at[b], device_id=(to, kv), device_id_type=MESH).start()

            def sends(i, _):
                k = lax.div(i + 1, 2)
                dz = Z // 2 + jnp.where(lax.rem(i, 2) == 1, -k, k)
                for dy in dys:
                    for dc in range(2):
                        send(dy, dz, dc)
                return 0

            lax.fori_loop(0, Z - 1, sends, 0)
            for dy in dys:
                for dc in range(2):
                    if (dy, dc) != (0, 0):
                        send(dy, 0, dc)
            if half == 0:
                @pl.when(b == 0)
                def _():
                    for dz in [0] + near:
                        for dy in second_half:
                            g1.along_y(dy, dz)
                            g1.core(dy, dz, c1.at[1])
            return 0

        lax.fori_loop(0, 2, unit, 0)
        if half == 0:
            g3.core(0, 0, c3)
            for dz in near:
                g3.along_z(dz)
                g3.core(0, dz, c3)
    for dz in [0] + near:
        for dy in range(1, Y):
            g3.along_y(dy, dz)
            g3.core(dy, dz, c3)
    g3.core_wait(Y * Z, c3)

    def widenkv(i, _):
        kv32[pl.ds(pl.multiple_of(i * 2 * kvr, 2 * kvr), 2 * kvr), :] = (
            bufkv[lax.div(i, 2 * Z), lax.rem(i, 2 * Z)].astype(F32))
        return 0

    lax.fori_loop(0, n, widenkv, 0)
    kk, vvv = [], []
    for g in range(2):
        kk.append(jnp.concatenate([kv32[pl.ds(2 * i + g, n, stride=2 * kvr), :] for i in range(rows)], axis=0))
        vvv.append(jnp.concatenate([kv32[pl.ds(kvr + 2 * i + g, n, stride=2 * kvr), :] for i in range(rows)], axis=0))
    ks = jnp.concatenate(kk, axis=1).astype(BF16)
    vs = jnp.concatenate(vvv, axis=1).astype(BF16)
    qf = q_ref[...].astype(F32)
    rid = lax.broadcasted_iota(jnp.int32, (qr, 128), 0)
    first = (lax.rem(rid, heads) < per).astype(F32)
    qo = jnp.concatenate([qf * first, qf * (1.0 - first)], axis=1).astype(BF16)
    sc = dot_t(qo, ks) * c2s
    kid = lax.broadcasted_iota(jnp.int32, (qr, np_), 1)
    key_pos = lax.rem(kid, n) * rows + lax.div(kid, n)
    row_pos = me * rows + lax.div(lax.broadcasted_iota(jnp.int32, (qr, np_), 0), heads)
    seen = key_pos <= row_pos
    sc = jnp.where(seen, sc, NEG)
    om = jnp.max(sc, axis=1, keepdims=True)
    ow = jnp.where(seen, jnp.exp2(sc - om), 0.0)
    ot = jnp.sum(ow, axis=1, keepdims=True)
    oo = dot(ow.astype(BF16), vs)
    own_o[...] = jnp.where(first > 0.5, oo[:, 0:128], oo[:, 128:256]) * (1.0 / ot)
    own_l[...] = jnp.broadcast_to(om + jnp.log2(ot), (qr, 128))

    for b in range(2):
        rest = pay.at[b, pl.ds(0, n - 1)]
        pltpu.make_async_remote_copy(src_ref=rest, dst_ref=rest, send_sem=asend, recv_sem=ar.at[b],
                                     device_id=(m.rank(0, 1, 0), kv), device_id_type=MESH).wait_recv()
        f32s[b * n * 16:(b + 1) * n * 16, :] = recv[b].reshape(n * 16, 128).astype(F32)
    st = sum(f32s[pl.ds(MOST * rows + i, 2 * n, stride=16), :] for i in range(rows))
    st = (st + pltpu.roll(st, 128 - 16, 1)) + pltpu.roll(st, 128 - 32, 1)
    st = st.T
    hid = lax.broadcasted_iota(jnp.int32, (heads, 2 * n), 0)
    for i in range(rows):
        at = pl.ds(i * heads, heads)
        own = own_l[at, 0:1]
        top = own
        xs_ = []
        for s in range(MOST):
            x = jnp.where(hm[s] == hid, st[s * rows + i:s * rows + i + 1, :], NEG)
            xs_.append(x)
            top = jnp.maximum(top, jnp.max(x, axis=1, keepdims=True))
        share = jnp.exp2(own - top)
        den = share
        num = share * own_o[at, :]
        for s in range(MOST):
            wt = jnp.exp2(xs_[s] - top)
            den = den + jnp.sum(wt, axis=1, keepdims=True)
            hi = wt.astype(BF16)
            lo = (wt - hi.astype(F32)).astype(BF16)
            r = f32s[pl.ds(s * rows + i, 2 * n, stride=16), :].astype(BF16)
            two = dot(jnp.concatenate([hi, lo], axis=0), r)
            num = num + (two[0:heads] + two[heads:2 * heads])
        a = (num / den).astype(BF16)
        att_ref[at, :] = a
        buf2[m.y, m.z, at, :] = a

    cut = qr - qr // 4
    g2 = GatherZ(m, buf2, pl.ds(0, cut), one_core, *sems[6:9])
    g4 = GatherY(m, buf2, pl.ds(cut, qr - cut), one_core, *sems[9:12])
    g4.start()
    g2.start()
    for i, dz in enumerate(near):
        g2.along_z(dz)
        if i == min(1, len(near) - 1):
            g4.forward()
    for dz in [0] + near:
        for dy in range(1, Y):
            g2.along_y(dy, dz)
    for dz in near:
        g4.across(dz)
    wcopy.wait()
    wgive.wait()
    share = Z * rows
    for dxs in (far_first(X)[:X // 2], far_first(X)[X // 2:]):
        for t, dx in enumerate(dxs):
            x = lax.rem(kv + dx, X)
            for j in range(Z):
                f32s[(t * Z + j) * qr:(t * Z + j + 1) * qr, :] = buf2[x, j].astype(F32)
        out = jnp.zeros((len(dxs) * share, 256), F32)
        for h in range(0, heads, 2):
            a = jnp.concatenate([f32s[pl.ds(h + e, len(dxs) * share, stride=heads), :] for e in range(2)], axis=1)
            at = slice(h * width, (h + 2) * width)
            out = out + dot(a.astype(BF16), jnp.concatenate([wv[0, at, :], wv[1, at, :]], axis=1))
        for t, dx in enumerate(dxs):
            x = lax.rem(kv + dx, X)
            mine = out[t * share:(t + 1) * share]
            halves = [mine[:, 0:128], mine[:, 128:256]]
            for dc in range(2):
                piece = jnp.where(lax.rem(m.c + dc, 2) == 0, halves[0], halves[1]).astype(BF16)
                if (dx, dc) == (0, 0):
                    part_ref[kv, m.c] = piece
                else:
                    k = 2 * dx + dc - 1
                    xp[k] = piece
                    pltpu.make_async_remote_copy(
                        src_ref=xp.at[k], dst_ref=part_ref.at[kv, m.c], send_sem=xs.at[k], recv_sem=xrs.at[k],
                        device_id=(m.rank(0, 0, dc), x), device_id_type=MESH).start()
    g1.drain(True)
    g3.drain(True)
    g2.drain(False)
    g4.drain()
    for b in range(2):
        rest = pay.at[b, pl.ds(0, n - 1)]
        pltpu.make_async_remote_copy(src_ref=rest, dst_ref=rest, send_sem=asend, recv_sem=ar.at[b],
                                     device_id=(m.rank(0, 1, 0), kv), device_id_type=MESH).wait_send()
    for dx in range(X):
        for dc in range(2):
            if (dx, dc) != (0, 0):
                k = 2 * dx + dc - 1
                pltpu.make_async_remote_copy(
                    src_ref=xp.at[k], dst_ref=part_ref.at[lax.rem(kv + X - dx, X), lax.rem(m.c + dc, 2)],
                    send_sem=xs.at[k], recv_sem=xrs.at[k],
                    device_id=(m.rank(0, 0, dc), lax.rem(kv + dx, X)), device_id_type=MESH).wait()


def close(att_ref, part_ref, a_ref, p_ref):
    a_ref[...] = att_ref[...]
    rows = p_ref.shape[0]
    sums = []
    for c in range(2):
        total = part_ref[0, c].astype(F32)
        for x in range(1, X):
            total = total + part_ref[x, c].astype(F32)
        sums.append(total.reshape(rows // 16, 8, 128))
    low = lax.broadcasted_iota(jnp.int32, sums[0].shape, 1) < 4
    even = jnp.where(low, sums[0], pltpu.roll(sums[1], 4, 1))
    odd = jnp.where(low, pltpu.roll(sums[0], 4, 1), sums[1])
    p_ref[...] = jnp.stack([even, odd], axis=1).reshape(rows, 128).astype(BF16)


def local(queries, span_keys, span_values, cache_keys, cache_values, gating, out_weight):
    rows, heads, width = queries.shape
    groups = span_keys.shape[1]
    n = Y * Z * 2
    np_ = n * rows
    qr = rows * heads
    kvr = rows * groups
    bp = BLOCK_POSITIONS
    raw = 2 * bp * groups
    part = min(1024, raw)
    unit = MOST * np_ // 2
    vm = pltpu.VMEM
    dma = pltpu.SemaphoreType.DMA
    along_z = [dma((Z - 1,)), dma((Z, Y - 1)), dma((3,))]
    along_y = [dma((Y - 1,)), dma((Z - 1,)), dma((3,))]
    scratch = [
        vm((raw, width), BF16), vm((raw, width), BF16),
        vm((2 * bp, width), BF16), vm((2 * bp, width), BF16), vm((2 * bp, width), BF16), vm((2 * bp, width), BF16),
        vm((2, *out_weight.shape), BF16),
        vm((Y, 2 * Z, qr, width), BF16), vm((Y, Z, qr, width), BF16), vm((Y, 2 * Z, 2 * kvr, width), BF16),
        vm((n * qr, width), F32), vm((n * 2 * kvr, width), F32), vm((part, width), F32),
        vm((2, unit, 2 * width), BF16),
        vm((2, unit, CHUNK), F32), vm((2, unit, width), F32), vm((2, unit, CHUNK), BF16), vm((2, unit, width), F32),
        vm((unit, 2 * width), F32), vm((unit, width), F32), vm((unit, width), F32),
        vm((MOST + 1, np_ // 2, width), F32), vm((n // 2 * 16, width), F32),
        vm((2, n, 16, width), BF16), vm((2, n, 16, width), BF16),
        vm((qr, width), F32), vm((qr, width), F32),
        vm((2 * X - 1, Z * rows, width), BF16),
        dma((3,)), dma((2,)), dma, dma((2 * X - 1,)), dma((2 * X - 1,)), dma, dma, dma((2,)), dma,
        *along_z, *along_z, *along_z, *along_y,
    ]
    inv = pl.BlockSpec(memory_space=pltpu.VMEM)
    anyw = pl.BlockSpec(memory_space=pl.ANY)
    att, parts = pl.pallas_call(
        kernel,
        out_shape=(jax.ShapeDtypeStruct((qr, width), BF16), jax.ShapeDtypeStruct((X, 2, Z * rows, width), BF16)),
        in_specs=[inv, inv, inv, inv, anyw, anyw, anyw],
        out_specs=(inv, inv),
        scratch_shapes=scratch,
        compiler_params=pltpu.CompilerParams(collective_id=0, has_side_effects=True, vmem_limit_bytes=60 << 20),
        name="sparse_attention",
    )(
        queries.reshape(qr, width), span_keys.reshape(kvr, width), span_values.reshape(kvr, width), gating,
        cache_keys.reshape(raw, width), cache_values.reshape(raw, width), out_weight,
    )
    att, proj = pl.pallas_call(
        close,
        out_shape=(jax.ShapeDtypeStruct((qr, width), BF16), jax.ShapeDtypeStruct((np_ // X, width), BF16)),
        in_specs=[inv, inv],
        out_specs=(inv, inv),
        name="close",
    )(att, parts)
    return att.reshape(rows, heads, width), proj


def solution(mesh):
    placed = (
        P("ctx", "kvh", None),
        P("ctx", "kvh", None),
        P("ctx", "kvh", None),
        P("ctx", "kvh", None),
        P("ctx", "kvh", None),
        P("kvh", None),
        P("kvh", "ctx"),
    )
    return jax.shard_map(
        local,
        mesh=mesh,
        in_specs=placed,
        out_specs=(P("ctx", "kvh", None), P("kvh", "ctx")),
        check_vma=False,
    )
```

```python
import functools

import jax
import jax.numpy as jnp
from jax import lax
from jax.experimental import pallas as pl
from jax.experimental.pallas import tpu as pltpu
from jax.sharding import PartitionSpec as P

Y, Z, X = 4, 8, 4
BLOCK_POSITIONS = 4096
MOST = 3
CHUNK = 2048
NEG = -1e30
MESH = pl.DeviceIdType.MESH
F32, BF16 = jnp.float32, jnp.bfloat16


def far_first(n):
    return sorted(range(n), key=lambda d: -min(d, n - d))


def near_first(n):
    return far_first(n)[:-1][::-1]


def dot_t(a, b):
    return lax.dot_general(a, b, (((1,), (1,)), ((), ())), preferred_element_type=F32)


def dot(a, b):
    return jnp.dot(a, b, preferred_element_type=F32)


class Comm:
    def __init__(self):
        self.me = lax.axis_index("ctx")
        self.kv = lax.axis_index("kvh")
        self.c = lax.rem(self.me, 2)
        self.z = lax.rem(lax.div(self.me, 2), Z)
        self.y = lax.div(self.me, 2 * Z)

    def rank(self, dy, dz, dc):
        return (lax.rem(self.y + dy, Y) * Z + lax.rem(self.z + dz, Z)) * 2 + lax.rem(self.c + dc, 2)

    def y_of(self, dy):
        return lax.rem(self.y + dy, Y)

    def copy(self, ref, send, recv, dy, dz, dc):
        return pltpu.make_async_remote_copy(src_ref=ref, dst_ref=ref, send_sem=send, recv_sem=recv,
                                            device_id=(self.rank(dy, dz, dc), self.kv), device_id_type=MESH)


class GatherZ:
    def __init__(self, m, buf, at, slot, zs, ys, sends, ahead=()):
        self.m, self.buf, self.at, self.slot = m, buf, at, slot
        self.zs, self.ys, self.sends = zs, ys, sends
        self.ahead = ahead or far_first(Y)[:-1]

    def ref(self, dy, dz):
        return self.buf.at[self.m.y_of(dy), self.slot(dz), self.at]

    def spread(self, dz):
        m = self.m
        for dy in self.ahead:
            m.copy(self.ref(0, Z - dz), self.sends.at[1], self.ys.at[dz, dy - 1], dy, 0, 0).start()

    def start(self):
        m = self.m
        for dz in near_first(Z):
            m.copy(self.ref(0, 0), self.sends.at[0], self.zs.at[dz - 1], 0, dz, 0).start()
        self.spread(0)

    def along_z(self, dz):
        self.m.copy(self.ref(0, Z - dz), self.sends.at[0], self.zs.at[dz - 1], 0, dz, 0).wait_recv()
        self.spread(dz)

    def along_y(self, dy, dz):
        self.m.copy(self.ref(dy, Z - dz), self.sends.at[1], self.ys.at[dz, Y - dy - 1], Y - dy, 0, 0).wait_recv()

    def core(self, dy, dz, sem):
        self.m.copy(self.ref(dy, Z - dz), self.sends.at[2], sem, 0, 0, 1).start()

    def core_wait(self, number, sem):
        shards = self.buf.at[pl.ds(0, number // Z), pl.ds(0, Z), self.at]
        self.m.copy(shards, self.sends.at[2], sem, 0, 0, 1).wait_recv()

    def drain(self, core):
        m = self.m
        parts = [self.buf.at[0, pl.ds(0, Z - 1), self.at], self.buf.at[pl.ds(0, Y - 1), pl.ds(0, Z), self.at]]
        if core:
            parts.append(self.buf.at[:, pl.ds(0, Z), self.at])
        for i, part in enumerate(parts):
            m.copy(part, self.sends.at[i], self.zs.at[0], 0, 0, 1).wait_send()


class GatherY:
    def __init__(self, m, buf, at, slot, ys, zs, sends):
        self.m, self.buf, self.at, self.slot = m, buf, at, slot
        self.ys, self.zs, self.sends = ys, zs, sends

    def start(self):
        m = self.m
        ref = self.buf.at[m.y, self.slot(0), self.at]
        for dy in far_first(Y)[:-1]:
            m.copy(ref, self.sends.at[0], self.ys.at[dy - 1], dy, 0, 0).start()

    def forward(self):
        m = self.m
        for dy in near_first(Y):
            ref = self.buf.at[m.y_of(Y - dy), self.slot(0), self.at]
            m.copy(ref, self.sends.at[0], self.ys.at[dy - 1], dy, 0, 0).wait_recv()
        for dz in far_first(Z)[:-1]:
            m.copy(self.buf.at[:, self.slot(0), self.at], self.sends.at[1], self.zs.at[dz - 1], 0, dz, 0).start()

    def across(self, dz):
        ref = self.buf.at[:, self.slot(Z - dz), self.at]
        self.m.copy(ref, self.sends.at[1], self.zs.at[dz - 1], 0, dz, 0).wait_recv()

    def drain(self):
        m = self.m
        m.copy(self.buf.at[0, pl.ds(0, Y - 1), self.at], self.sends.at[0], self.zs.at[0], 0, 0, 1).wait_send()
        m.copy(self.buf.at[:, pl.ds(0, Z - 1), self.at], self.sends.at[1], self.zs.at[0], 0, 0, 1).wait_send()


def kernel(q_ref, sk_ref, sv_ref, gat_ref, kc_ref, vc_ref, w_ref, att_ref, part_ref,
           kraw, vraw, k0, k1, v0, v1, wv, buf, buf2, bufkv, f32s, kv32, d32, qaug,
           sb, cm, pb, alb, acc, mm, ll, ob, pf, pay, recv, own_o, own_l, xp,
           loc, wl, ar, asend, xs, xrs, ws, wrs, c1, c3, *sems):
    m = Comm()
    zc = 2 * m.z + m.c

    def both_cores(dz):
        return 2 * lax.rem(m.z + dz, Z) + m.c

    def one_core(dz):
        return lax.rem(m.z + dz, Z)

    n = Y * Z * 2
    me, kv = m.me, m.kv
    heads, topk = gat_ref.shape
    rows = q_ref.shape[0] // heads
    per = heads // 2
    width = q_ref.shape[1]
    bp = BLOCK_POSITIONS
    np_ = n * rows
    qr = rows * heads
    kvr = sk_ref.shape[0]
    row = 2 * Z * rows
    hp = Y // 2 * row
    c2s = width ** -0.5 * 1.4426950408889634

    wcopy = pltpu.make_async_copy(w_ref, wv.at[m.c], wl)
    wgive = pltpu.make_async_remote_copy(src_ref=w_ref, dst_ref=wv.at[m.c], send_sem=ws, recv_sem=wrs,
                                         device_id=(m.rank(0, 0, 1), kv), device_id_type=MESH)
    bar = pltpu.get_barrier_semaphore()
    for dz in far_first(Z)[:-1]:
        pl.semaphore_signal(bar, inc=1, device_id=(m.rank(0, dz, 0), kv), device_id_type=MESH)
    for dy in far_first(Y)[:-1]:
        pl.semaphore_signal(bar, inc=1, device_id=(m.rank(dy, 0, 0), kv), device_id_type=MESH)
    for dx in range(X):
        for dc in range(2):
            if (dx, dc) != (0, 0):
                pl.semaphore_signal(bar, inc=1, device_id=(m.rank(0, 0, dc), lax.rem(kv + dx, X)), device_id_type=MESH)
    buf[m.y, zc] = q_ref[...]
    bufkv[m.y, zc] = jnp.concatenate([sk_ref[...], sv_ref[...]], axis=0)

    lane = lax.broadcasted_iota(jnp.int32, (heads, 2 * n), 1)
    block_of = lax.rem(lane, n) * 2 + lax.div(lane, n)
    gat = gat_ref[...]
    chosen = jnp.zeros((heads, 2 * n), jnp.int32)
    for t in range(topk):
        chosen = jnp.maximum(chosen, (gat[:, t:t + 1] == block_of).astype(jnp.int32))
    count = jnp.zeros((1, 2 * n), jnp.int32)
    hm = [jnp.full((1, 2 * n), -1, jnp.int32) for _ in range(MOST)]
    for h in range(heads):
        ch = chosen[h:h + 1, :]
        for s in range(MOST):
            hm[s] = jnp.where((ch == 1) & (count == s), h, hm[s])
        count = count + ch
    lane1 = lax.broadcasted_iota(jnp.int32, (1, 2 * n), 1)
    own_heads = [[jnp.maximum(jnp.max(jnp.where(lane1 == b * n + me, hm[s], -1)), 0) for s in range(MOST)]
                 for b in range(2)]

    part = d32.shape[0]
    parts = kraw.shape[0] // part
    order = [(a, blk * (parts // 2) + i) for blk in range(2) for a in range(2) for i in range(parts // 2)]
    arrays = ((kc_ref, kraw, k0, k1), (vc_ref, vraw, v0, v1))

    def load(j):
        a, i = order[j]
        at = pl.ds(i * part, part)
        return pltpu.make_async_copy(arrays[a][0].at[at], arrays[a][1].at[at], loc.at[j])

    def pieces():
        for j, (a, i) in enumerate(order):
            load(j).wait()
            _, raw, even, odd = arrays[a]
            to = pl.ds(i * (part // 2), part // 2)
            d32[...] = raw[pl.ds(i * part, part), :].astype(F32)
            even[to, :] = d32[pl.ds(0, part // 2, stride=2), :].astype(BF16)
            odd[to, :] = d32[pl.ds(1, part // 2, stride=2), :].astype(BF16)
            yield

    work = pieces()

    def beside(number):
        for _ in range(number):
            next(work, None)

    for j in range(len(order)):
        load(j).start()
    beside(2)
    pl.semaphore_wait(bar, Z - 1 + Y - 1 + 2 * X - 1)

    near = near_first(Z)
    g1 = GatherZ(m, buf, pl.ds(0, qr), both_cores, sems[0], sems[1], sems[2], ahead=range(Y - 1, 0, -1))
    g1.start()
    g1.core(0, 0, c1.at[0])
    beside(len(order) * 3 // 8)
    for dz in near:
        g1.along_z(dz)
        g1.core(0, dz, c1.at[0])
    first_half = list(range(1, Y // 2))
    second_half = list(range(Y // 2, Y))
    beside(len(order) * 3 // 8)
    for dz in [0] + near:
        for dy in first_half:
            g1.along_y(dy, dz)
            g1.core(dy, dz, c1.at[0])
    beside(len(order))
    wcopy.start()
    g1.core_wait(Y * Z // 2, c1.at[0])
    wgive.start()
    g3 = GatherZ(m, bufkv, pl.ds(0, 2 * kvr), both_cores, sems[3], sems[4], sems[5])
    g3.start()

    nb = bp // CHUNK

    def rows_of(half):
        return list(range(half * (Y // 2), (half + 1) * (Y // 2)))

    def prepare(half):
        for dy in rows_of(half):
            yy = m.y_of(dy)

            def widen(i, _):
                f32s[pl.ds(pl.multiple_of((yy * (2 * Z) + i) * qr, qr), qr), :] = buf[yy, i].astype(F32)
                return 0

            lax.fori_loop(0, 2 * Z, widen, 0)
        for b in range(2):
            for s in range(MOST):
                h = own_heads[b][s]
                first = (h < per).astype(F32)
                for t, dy in enumerate(rows_of(half)):
                    qh = f32s[pl.ds(m.y_of(dy) * (row * heads) + h, row, stride=heads), :]
                    qaug[2 * half + b, s * hp + t * row:s * hp + (t + 1) * row, :] = jnp.concatenate(
                        [qh * first, qh * (1.0 - first)], axis=1).astype(BF16)

    def both(even, odd, g):
        at = pl.ds((g // nb % 2) * bp + g % nb * CHUNK, CHUNK)
        return jnp.concatenate([even[at, :], odd[at, :]], axis=1)

    def score(g):
        s = dot_t(qaug[g // nb], both(k0, k1, g))
        sb[g % 2] = s
        top = s[:, :128]
        for j in range(1, CHUNK // 128):
            top = jnp.maximum(top, s[:, j * 128:(j + 1) * 128])
        cm[g % 2] = top

    def soften(g):
        u, slot = g // nb % 2, g % 2
        m1 = jnp.max(cm[slot], axis=1, keepdims=True) * c2s
        if g % nb:
            m0 = mm[u]
            m1 = jnp.maximum(m0, m1)
            al = jnp.exp2(m0 - m1)
            alb[slot] = al
        else:
            m1 = jnp.broadcast_to(m1, (MOST * hp, 128))
        p = jnp.exp2(sb[slot] * c2s - m1[:, :1])
        ps = p[:, :128]
        for j in range(1, CHUNK // 128):
            ps = ps + p[:, j * 128:(j + 1) * 128]
        ll[u] = ll[u] * al + ps if g % nb else ps
        mm[u] = m1
        pb[slot] = p.astype(BF16)

    def gain(g):
        u, slot = g // nb % 2, g % 2
        o = dot(pb[slot], both(v0, v1, g))
        if g % nb:
            al = alb[slot]
            acc[u] = acc[u] * jnp.concatenate([al, al], axis=1) + o
        else:
            acc[u] = o

    def pack(unit):
        u, b = unit % 2, unit % 2
        ln = lax.broadcasted_iota(jnp.int32, (hp, 128), 1)
        rw = lax.rem(lax.broadcasted_iota(jnp.int32, (hp, 128), 0), rows)
        stat = jnp.zeros((hp, 128), F32)
        for s in range(MOST):
            sl = pl.ds(s * hp, hp)
            tot = jnp.sum(ll[u, sl, :], axis=1, keepdims=True)
            lse = mm[u, sl, :] + jnp.log2(tot)
            first = own_heads[b][s] < per
            ob[s] = jnp.where(first, acc[u, sl, 0:128], acc[u, sl, 128:256]) * (1.0 / tot)
            hi = lse.astype(BF16).astype(F32)
            mid = (lse - hi).astype(BF16).astype(F32)
            lo = (lse - hi) - mid
            val = jnp.where(ln < 16, hi, jnp.where(ln < 32, mid, lo))
            stat = jnp.where((lax.rem(ln, 16) == s * rows + rw) & (ln < 48), val, stat)
        ob[MOST] = stat
        for t, dy in enumerate(rows_of(unit // 2)):
            for j in range(Z):
                d = t * 2 * Z + 2 * j
                for s in range(MOST + 1):
                    x = ob[s, d * rows:(d + 2) * rows, :]
                    pf[d * 16 + s * rows:d * 16 + (s + 1) * rows, :] = x[0:rows]
                    pf[(d + 1) * 16 + s * rows:(d + 1) * 16 + (s + 1) * rows, :] = x[rows:2 * rows]
            of_y = pf[t * 2 * Z * 16:(t + 1) * 2 * Z * 16, :].astype(BF16).reshape(2 * Z, 16, 128)
            pay[b, pl.ds(m.y_of(dy) * (2 * Z), 2 * Z)] = of_y
        if unit // 2 == 0:
            recv[b, me] = pay[b, me]

    def give(unit):
        b = unit % 2
        dys = rows_of(unit // 2)

        def send(dy, dz, dc):
            to = m.rank(dy, dz, dc)
            pltpu.make_async_remote_copy(src_ref=pay.at[b, to], dst_ref=recv.at[b, me], send_sem=asend,
                                         recv_sem=ar.at[b], device_id=(to, kv), device_id_type=MESH).start()

        def sends(i, _):
            k = lax.div(i + 1, 2)
            dz = Z // 2 + jnp.where(lax.rem(i, 2) == 1, -k, k)
            for dy in dys:
                for dc in range(2):
                    send(dy, dz, dc)
            return 0

        lax.fori_loop(0, Z - 1, sends, 0)
        for dy in dys:
            for dc in range(2):
                if (dy, dc) != (0, 0):
                    send(dy, 0, dc)

    prepare(0)
    score(0)
    for g in range(4 * nb + 1):
        if g + 1 == 2 * nb:
            g1.core_wait(Y * Z // 2, c1.at[1])
            prepare(1)
        if g < 4 * nb:
            soften(g)
        if g >= 1:
            gain(g - 1)
        if g + 1 < 4 * nb:
            score(g + 1)
        if g >= 1 and g % nb == 0:
            pack(g // nb - 1)
            give(g // nb - 1)
        if g == nb - 1:
            for dz in [0] + near:
                for dy in second_half:
                    g1.along_y(dy, dz)
                    g1.core(dy, dz, c1.at[1])
        if g == 2 * nb:
            g3.core(0, 0, c3)
            for dz in near:
                g3.along_z(dz)
                g3.core(0, dz, c3)
    for dz in [0] + near:
        for dy in range(1, Y):
            g3.along_y(dy, dz)
            g3.core(dy, dz, c3)
    g3.core_wait(Y * Z, c3)

    def widenkv(i, _):
        kv32[pl.ds(pl.multiple_of(i * 2 * kvr, 2 * kvr), 2 * kvr), :] = (
            bufkv[lax.div(i, 2 * Z), lax.rem(i, 2 * Z)].astype(F32))
        return 0

    lax.fori_loop(0, n, widenkv, 0)
    kk, vvv = [], []
    for g in range(2):
        kk.append(jnp.concatenate([kv32[pl.ds(2 * i + g, n, stride=2 * kvr), :] for i in range(rows)], axis=0))
        vvv.append(jnp.concatenate([kv32[pl.ds(kvr + 2 * i + g, n, stride=2 * kvr), :] for i in range(rows)], axis=0))
    ks = jnp.concatenate(kk, axis=1).astype(BF16)
    vs = jnp.concatenate(vvv, axis=1).astype(BF16)
    qf = q_ref[...].astype(F32)
    rid = lax.broadcasted_iota(jnp.int32, (qr, 128), 0)
    first = (lax.rem(rid, heads) < per).astype(F32)
    qo = jnp.concatenate([qf * first, qf * (1.0 - first)], axis=1).astype(BF16)
    sc = dot_t(qo, ks) * c2s
    kid = lax.broadcasted_iota(jnp.int32, (qr, np_), 1)
    key_pos = lax.rem(kid, n) * rows + lax.div(kid, n)
    row_pos = me * rows + lax.div(lax.broadcasted_iota(jnp.int32, (qr, np_), 0), heads)
    seen = key_pos <= row_pos
    sc = jnp.where(seen, sc, NEG)
    om = jnp.max(sc, axis=1, keepdims=True)
    ow = jnp.where(seen, jnp.exp2(sc - om), 0.0)
    ot = jnp.sum(ow, axis=1, keepdims=True)
    oo = dot(ow.astype(BF16), vs)
    own_o[...] = jnp.where(first > 0.5, oo[:, 0:128], oo[:, 128:256]) * (1.0 / ot)
    own_l[...] = jnp.broadcast_to(om + jnp.log2(ot), (qr, 128))

    for b in range(2):
        rest = pay.at[b, pl.ds(0, n - 1)]
        pltpu.make_async_remote_copy(src_ref=rest, dst_ref=rest, send_sem=asend, recv_sem=ar.at[b],
                                     device_id=(m.rank(0, 1, 0), kv), device_id_type=MESH).wait_recv()
        f32s[b * n * 16:(b + 1) * n * 16, :] = recv[b].reshape(n * 16, 128).astype(F32)
    st = sum(f32s[pl.ds(MOST * rows + i, 2 * n, stride=16), :] for i in range(rows))
    st = (st + pltpu.roll(st, 128 - 16, 1)) + pltpu.roll(st, 128 - 32, 1)
    st = st.T
    hid = lax.broadcasted_iota(jnp.int32, (heads, 2 * n), 0)
    for i in range(rows):
        at = pl.ds(i * heads, heads)
        own = own_l[at, 0:1]
        top = own
        xs_ = []
        for s in range(MOST):
            x = jnp.where(hm[s] == hid, st[s * rows + i:s * rows + i + 1, :], NEG)
            xs_.append(x)
            top = jnp.maximum(top, jnp.max(x, axis=1, keepdims=True))
        share = jnp.exp2(own - top)
        den = share
        num = share * own_o[at, :]
        for s in range(MOST):
            wt = jnp.exp2(xs_[s] - top)
            den = den + jnp.sum(wt, axis=1, keepdims=True)
            hi = wt.astype(BF16)
            lo = (wt - hi.astype(F32)).astype(BF16)
            r = f32s[pl.ds(s * rows + i, 2 * n, stride=16), :].astype(BF16)
            two = dot(jnp.concatenate([hi, lo], axis=0), r)
            num = num + (two[0:heads] + two[heads:2 * heads])
        a = (num / den).astype(BF16)
        att_ref[at, :] = a
        buf2[m.y, m.z, at, :] = a

    cut = qr - qr // 4
    g2 = GatherZ(m, buf2, pl.ds(0, cut), one_core, *sems[6:9])
    g4 = GatherY(m, buf2, pl.ds(cut, qr - cut), one_core, *sems[9:12])
    g4.start()
    g2.start()
    for i, dz in enumerate(near):
        g2.along_z(dz)
        if i == min(1, len(near) - 1):
            g4.forward()
    for dz in [0] + near:
        for dy in range(1, Y):
            g2.along_y(dy, dz)
    for dz in near:
        g4.across(dz)
    wcopy.wait()
    wgive.wait()
    share = Z * rows
    for dxs in (far_first(X)[:X // 2], far_first(X)[X // 2:]):
        for t, dx in enumerate(dxs):
            x = lax.rem(kv + dx, X)
            for j in range(Z):
                f32s[(t * Z + j) * qr:(t * Z + j + 1) * qr, :] = buf2[x, j].astype(F32)
        out = jnp.zeros((len(dxs) * share, 256), F32)
        for h in range(0, heads, 2):
            a = jnp.concatenate([f32s[pl.ds(h + e, len(dxs) * share, stride=heads), :] for e in range(2)], axis=1)
            at = slice(h * width, (h + 2) * width)
            out = out + dot(a.astype(BF16), jnp.concatenate([wv[0, at, :], wv[1, at, :]], axis=1))
        for t, dx in enumerate(dxs):
            x = lax.rem(kv + dx, X)
            mine = out[t * share:(t + 1) * share]
            halves = [mine[:, 0:128], mine[:, 128:256]]
            for dc in range(2):
                piece = jnp.where(lax.rem(m.c + dc, 2) == 0, halves[0], halves[1]).astype(BF16)
                if (dx, dc) == (0, 0):
                    part_ref[kv, m.c] = piece
                else:
                    k = 2 * dx + dc - 1
                    xp[k] = piece
                    pltpu.make_async_remote_copy(
                        src_ref=xp.at[k], dst_ref=part_ref.at[kv, m.c], send_sem=xs.at[k], recv_sem=xrs.at[k],
                        device_id=(m.rank(0, 0, dc), x), device_id_type=MESH).start()
    g1.drain(True)
    g3.drain(True)
    g2.drain(False)
    g4.drain()
    for b in range(2):
        rest = pay.at[b, pl.ds(0, n - 1)]
        pltpu.make_async_remote_copy(src_ref=rest, dst_ref=rest, send_sem=asend, recv_sem=ar.at[b],
                                     device_id=(m.rank(0, 1, 0), kv), device_id_type=MESH).wait_send()
    for dx in range(X):
        for dc in range(2):
            if (dx, dc) != (0, 0):
                k = 2 * dx + dc - 1
                pltpu.make_async_remote_copy(
                    src_ref=xp.at[k], dst_ref=part_ref.at[lax.rem(kv + X - dx, X), lax.rem(m.c + dc, 2)],
                    send_sem=xs.at[k], recv_sem=xrs.at[k],
                    device_id=(m.rank(0, 0, dc), lax.rem(kv + dx, X)), device_id_type=MESH).wait()


def close(att_ref, part_ref, a_ref, p_ref):
    a_ref[...] = att_ref[...]
    rows = p_ref.shape[0]
    sums = []
    for c in range(2):
        total = part_ref[0, c].astype(F32)
        for x in range(1, X):
            total = total + part_ref[x, c].astype(F32)
        sums.append(total.reshape(rows // 16, 8, 128))
    low = lax.broadcasted_iota(jnp.int32, sums[0].shape, 1) < 4
    even = jnp.where(low, sums[0], pltpu.roll(sums[1], 4, 1))
    odd = jnp.where(low, pltpu.roll(sums[0], 4, 1), sums[1])
    p_ref[...] = jnp.stack([even, odd], axis=1).reshape(rows, 128).astype(BF16)


def local(queries, span_keys, span_values, cache_keys, cache_values, gating, out_weight):
    rows, heads, width = queries.shape
    groups = span_keys.shape[1]
    n = Y * Z * 2
    np_ = n * rows
    qr = rows * heads
    kvr = rows * groups
    bp = BLOCK_POSITIONS
    raw = 2 * bp * groups
    part = min(1024, raw // 2)
    unit = MOST * np_ // 2
    vm = pltpu.VMEM
    dma = pltpu.SemaphoreType.DMA
    along_z = [dma((Z - 1,)), dma((Z, Y - 1)), dma((3,))]
    along_y = [dma((Y - 1,)), dma((Z - 1,)), dma((3,))]
    scratch = [
        vm((raw, width), BF16), vm((raw, width), BF16),
        vm((2 * bp, width), BF16), vm((2 * bp, width), BF16), vm((2 * bp, width), BF16), vm((2 * bp, width), BF16),
        vm((2, *out_weight.shape), BF16),
        vm((Y, 2 * Z, qr, width), BF16), vm((Y, Z, qr, width), BF16), vm((Y, 2 * Z, 2 * kvr, width), BF16),
        vm((n * qr, width), F32), vm((n * 2 * kvr, width), F32), vm((part, width), F32),
        vm((4, unit, 2 * width), BF16),
        vm((2, unit, CHUNK), F32), vm((2, unit, width), F32), vm((2, unit, CHUNK), BF16), vm((2, unit, width), F32),
        vm((2, unit, 2 * width), F32), vm((2, unit, width), F32), vm((2, unit, width), F32),
        vm((MOST + 1, np_ // 2, width), F32), vm((n // 2 * 16, width), F32),
        vm((2, n, 16, width), BF16), vm((2, n, 16, width), BF16),
        vm((qr, width), F32), vm((qr, width), F32),
        vm((2 * X - 1, Z * rows, width), BF16),
        dma((2 * (raw // part),)), dma, dma((2,)), dma, dma((2 * X - 1,)), dma((2 * X - 1,)), dma, dma, dma((2,)), dma,
        *along_z, *along_z, *along_z, *along_y,
    ]
    inv = pl.BlockSpec(memory_space=pltpu.VMEM)
    anyw = pl.BlockSpec(memory_space=pl.ANY)
    att, parts = pl.pallas_call(
        kernel,
        out_shape=(jax.ShapeDtypeStruct((qr, width), BF16), jax.ShapeDtypeStruct((X, 2, Z * rows, width), BF16)),
        in_specs=[inv, inv, inv, inv, anyw, anyw, anyw],
        out_specs=(inv, inv),
        scratch_shapes=scratch,
        compiler_params=pltpu.CompilerParams(collective_id=0, has_side_effects=True, vmem_limit_bytes=60 << 20),
        name="sparse_attention",
    )(
        queries.reshape(qr, width), span_keys.reshape(kvr, width), span_values.reshape(kvr, width), gating,
        cache_keys.reshape(raw, width), cache_values.reshape(raw, width), out_weight,
    )
    att, proj = pl.pallas_call(
        close,
        out_shape=(jax.ShapeDtypeStruct((qr, width), BF16), jax.ShapeDtypeStruct((np_ // X, width), BF16)),
        in_specs=[inv, inv],
        out_specs=(inv, inv),
        name="close",
    )(att, parts)
    return att.reshape(rows, heads, width), proj


def solution(mesh):
    placed = (
        P("ctx", "kvh", None),
        P("ctx", "kvh", None),
        P("ctx", "kvh", None),
        P("ctx", "kvh", None),
        P("ctx", "kvh", None),
        P("kvh", None),
        P("kvh", "ctx"),
    )
    return jax.shard_map(
        local,
        mesh=mesh,
        in_specs=placed,
        out_specs=(P("ctx", "kvh", None), P("kvh", "ctx")),
        check_vma=False,
    )
```

```python
import functools

import jax
import jax.numpy as jnp
from jax import lax
from jax.experimental import pallas as pl
from jax.experimental.pallas import tpu as pltpu
from jax.sharding import PartitionSpec as P

Y, Z, X = 4, 8, 4
BLOCK_POSITIONS = 4096
MOST = 3
CHUNK = 1024
NEG = -1e30
MESH = pl.DeviceIdType.MESH
F32, BF16 = jnp.float32, jnp.bfloat16


def far_first(n):
    return sorted(range(n), key=lambda d: -min(d, n - d))


def near_first(n):
    return far_first(n)[:-1][::-1]


def dot_t(a, b):
    return lax.dot_general(a, b, (((1,), (1,)), ((), ())), preferred_element_type=F32)


def dot(a, b):
    return jnp.dot(a, b, preferred_element_type=F32)


class Comm:
    def __init__(self):
        self.me = lax.axis_index("ctx")
        self.kv = lax.axis_index("kvh")
        self.c = lax.rem(self.me, 2)
        self.z = lax.rem(lax.div(self.me, 2), Z)
        self.y = lax.div(self.me, 2 * Z)

    def rank(self, dy, dz, dc):
        return (lax.rem(self.y + dy, Y) * Z + lax.rem(self.z + dz, Z)) * 2 + lax.rem(self.c + dc, 2)

    def y_of(self, dy):
        return lax.rem(self.y + dy, Y)

    def copy(self, ref, send, recv, dy, dz, dc):
        return pltpu.make_async_remote_copy(src_ref=ref, dst_ref=ref, send_sem=send, recv_sem=recv,
                                            device_id=(self.rank(dy, dz, dc), self.kv), device_id_type=MESH)


class GatherZ:
    def __init__(self, m, buf, at, slot, zs, ys, sends, ahead=()):
        self.m, self.buf, self.at, self.slot = m, buf, at, slot
        self.zs, self.ys, self.sends = zs, ys, sends
        self.ahead = ahead or far_first(Y)[:-1]

    def ref(self, dy, dz):
        return self.buf.at[self.m.y_of(dy), self.slot(dz), self.at]

    def spread(self, dz):
        m = self.m
        for dy in self.ahead:
            m.copy(self.ref(0, Z - dz), self.sends.at[1], self.ys.at[dz, dy - 1], dy, 0, 0).start()

    def start(self):
        m = self.m
        for dz in near_first(Z):
            m.copy(self.ref(0, 0), self.sends.at[0], self.zs.at[dz - 1], 0, dz, 0).start()
        self.spread(0)

    def along_z(self, dz):
        self.m.copy(self.ref(0, Z - dz), self.sends.at[0], self.zs.at[dz - 1], 0, dz, 0).wait_recv()
        self.spread(dz)

    def along_y(self, dy, dz):
        self.m.copy(self.ref(dy, Z - dz), self.sends.at[1], self.ys.at[dz, Y - dy - 1], Y - dy, 0, 0).wait_recv()

    def core(self, dy, dz, sem):
        self.m.copy(self.ref(dy, Z - dz), self.sends.at[2], sem, 0, 0, 1).start()

    def core_wait(self, number, sem):
        shards = self.buf.at[pl.ds(0, number // Z), pl.ds(0, Z), self.at]
        self.m.copy(shards, self.sends.at[2], sem, 0, 0, 1).wait_recv()

    def drain(self, core):
        m = self.m
        parts = [self.buf.at[0, pl.ds(0, Z - 1), self.at], self.buf.at[pl.ds(0, Y - 1), pl.ds(0, Z), self.at]]
        if core:
            parts.append(self.buf.at[:, pl.ds(0, Z), self.at])
        for i, part in enumerate(parts):
            m.copy(part, self.sends.at[i], self.zs.at[0], 0, 0, 1).wait_send()


class GatherY:
    def __init__(self, m, buf, at, slot, ys, zs, sends):
        self.m, self.buf, self.at, self.slot = m, buf, at, slot
        self.ys, self.zs, self.sends = ys, zs, sends

    def start(self):
        m = self.m
        ref = self.buf.at[m.y, self.slot(0), self.at]
        for dy in far_first(Y)[:-1]:
            m.copy(ref, self.sends.at[0], self.ys.at[dy - 1], dy, 0, 0).start()

    def forward(self):
        m = self.m
        for dy in near_first(Y):
            ref = self.buf.at[m.y_of(Y - dy), self.slot(0), self.at]
            m.copy(ref, self.sends.at[0], self.ys.at[dy - 1], dy, 0, 0).wait_recv()
        for dz in far_first(Z)[:-1]:
            m.copy(self.buf.at[:, self.slot(0), self.at], self.sends.at[1], self.zs.at[dz - 1], 0, dz, 0).start()

    def across(self, dz):
        ref = self.buf.at[:, self.slot(Z - dz), self.at]
        self.m.copy(ref, self.sends.at[1], self.zs.at[dz - 1], 0, dz, 0).wait_recv()

    def drain(self):
        m = self.m
        m.copy(self.buf.at[0, pl.ds(0, Y - 1), self.at], self.sends.at[0], self.zs.at[0], 0, 0, 1).wait_send()
        m.copy(self.buf.at[:, pl.ds(0, Z - 1), self.at], self.sends.at[1], self.zs.at[0], 0, 0, 1).wait_send()


def kernel(q_ref, sk_ref, sv_ref, gat_ref, kc_ref, vc_ref, w_ref, att_ref, part_ref,
           kraw, vraw, k0, k1, v0, v1, wv, qpay, qrecv, buf2, bufkv, f32s, kv32, d32, qaug,
           sb, cm, pb, alb, acc, mm, ll, ob, pf, pay, recv, own_o, own_l, xp,
           loc, wl, ar, asend, xs, xrs, ws, wrs, qs, qrs, c3, *sems):
    m = Comm()
    zc = 2 * m.z + m.c

    def both_cores(dz):
        return 2 * lax.rem(m.z + dz, Z) + m.c

    def one_core(dz):
        return lax.rem(m.z + dz, Z)

    n = Y * Z * 2
    me, kv = m.me, m.kv
    heads, topk = gat_ref.shape
    rows = q_ref.shape[0] // heads
    per = heads // 2
    width = q_ref.shape[1]
    bp = BLOCK_POSITIONS
    np_ = n * rows
    qr = rows * heads
    kvr = sk_ref.shape[0]
    row = 2 * Z * rows
    hp = Y // 2 * row
    c2s = width ** -0.5 * 1.4426950408889634

    wcopy = pltpu.make_async_copy(w_ref, wv.at[m.c], wl)
    wgive = pltpu.make_async_remote_copy(src_ref=w_ref, dst_ref=wv.at[m.c], send_sem=ws, recv_sem=wrs,
                                         device_id=(m.rank(0, 0, 1), kv), device_id_type=MESH)
    bar = pltpu.get_barrier_semaphore()

    def greet(i, _):
        pl.semaphore_signal(bar, inc=1, device_id=(lax.rem(me + i, n), kv), device_id_type=MESH)
        return 0

    lax.fori_loop(1, n, greet, 0)
    for dx in range(1, X):
        for dc in range(2):
            pl.semaphore_signal(bar, inc=1, device_id=(m.rank(0, 0, dc), lax.rem(kv + dx, X)), device_id_type=MESH)
    bufkv[m.y, zc] = jnp.concatenate([sk_ref[...], sv_ref[...]], axis=0)

    lane = lax.broadcasted_iota(jnp.int32, (heads, 2 * n), 1)
    block_of = lax.rem(lane, n) * 2 + lax.div(lane, n)
    gat = gat_ref[...]
    chosen = jnp.zeros((heads, 2 * n), jnp.int32)
    for t in range(topk):
        chosen = jnp.maximum(chosen, (gat[:, t:t + 1] == block_of).astype(jnp.int32))
    count = jnp.zeros((1, 2 * n), jnp.int32)
    hm = [jnp.full((1, 2 * n), -1, jnp.int32) for _ in range(MOST)]
    for h in range(heads):
        ch = chosen[h:h + 1, :]
        for s in range(MOST):
            hm[s] = jnp.where((ch == 1) & (count == s), h, hm[s])
        count = count + ch
    lane1 = lax.broadcasted_iota(jnp.int32, (1, 2 * n), 1)
    own_heads = [[jnp.maximum(jnp.max(jnp.where(lane1 == b * n + me, hm[s], -1)), 0) for s in range(MOST)]
                 for b in range(2)]

    part = d32.shape[0]
    parts = kraw.shape[0] // part
    order = [(a, blk * (parts // 2) + i) for blk in range(2) for a in range(2) for i in range(parts // 2)]
    arrays = ((kc_ref, kraw, k0, k1), (vc_ref, vraw, v0, v1))

    def load(j):
        a, i = order[j]
        at = pl.ds(i * part, part)
        return pltpu.make_async_copy(arrays[a][0].at[at], arrays[a][1].at[at], loc.at[j])

    def pieces():
        for j, (a, i) in enumerate(order):
            load(j).wait()
            _, raw, even, odd = arrays[a]
            to = pl.ds(i * (part // 2), part // 2)
            d32[...] = raw[pl.ds(i * part, part), :].astype(F32)
            even[to, :] = d32[pl.ds(0, part // 2, stride=2), :].astype(BF16)
            odd[to, :] = d32[pl.ds(1, part // 2, stride=2), :].astype(BF16)
            yield

    work = pieces()

    def beside(number):
        for _ in range(number):
            next(work, None)

    for j in range(len(order)):
        load(j).start()
    f32s[0:2 * n * 16, :] = jnp.zeros((2 * n * 16, 128), F32)
    spot = lax.broadcasted_iota(jnp.int32, (128, 2 * n), 0)
    q_all = jnp.concatenate([q_ref[...], jnp.zeros((128 - qr, width), BF16)], axis=0)
    for s in range(MOST):
        for i in range(rows):
            pick = (spot == hm[s] + i * heads) & (hm[s] >= 0)
            f32s[pl.ds(s * rows + i, 2 * n, stride=16), :] = dot(pick.astype(F32).T.astype(BF16), q_all)
    for b in range(2):
        qpay[b] = f32s[b * n * 16:(b + 1) * n * 16, :].astype(BF16).reshape(n, 16, 128)
        qrecv[b, me] = qpay[b, me]
    pl.semaphore_wait(bar, n - 1 + 2 * (X - 1))
    near = near_first(Z)

    def to_all(b, dys, source, target, send_sem, recv_sem):
        def send(dy, dz, dc):
            to = m.rank(dy, dz, dc)
            pltpu.make_async_remote_copy(src_ref=source.at[b, to], dst_ref=target.at[b, me], send_sem=send_sem,
                                         recv_sem=recv_sem.at[b], device_id=(to, kv), device_id_type=MESH).start()

        def sends(i, _):
            k = lax.div(i + 1, 2)
            dz = Z // 2 + jnp.where(lax.rem(i, 2) == 1, -k, k)
            for dy in dys:
                for dc in range(2):
                    send(dy, dz, dc)
            return 0

        lax.fori_loop(0, Z - 1, sends, 0)
        for dy in dys:
            for dc in range(2):
                if (dy, dc) != (0, 0):
                    send(dy, 0, dc)

    def rest_of(b, source, send_sem, recv_sem):
        rest = source.at[b, pl.ds(0, n - 1)]
        return pltpu.make_async_remote_copy(src_ref=rest, dst_ref=rest, send_sem=send_sem, recv_sem=recv_sem.at[b],
                                            device_id=(m.rank(0, 1, 0), kv), device_id_type=MESH)

    for b in range(2):
        to_all(b, far_first(Y), qpay, qrecv, qs, qrs)
    beside(len(order))
    wcopy.start()
    wgive.start()
    g3 = GatherZ(m, bufkv, pl.ds(0, 2 * kvr), both_cores, *sems[0:3])
    g3.start()

    nb = bp // CHUNK

    def rows_of(half):
        return far_first(Y)[half * (Y // 2):(half + 1) * (Y // 2)]

    def prepare(b):
        rest_of(b, qpay, qs, qrs).wait_recv()
        f32s[0:n * 16, :] = qrecv[b].reshape(n * 16, 128).astype(F32)
        for half in range(2):
            for s in range(MOST):
                first = (own_heads[b][s] < per).astype(F32)
                for i in range(rows):
                    for t, dy in enumerate(rows_of(half)):
                        qh = f32s[pl.ds(m.y_of(dy) * (2 * Z * 16) + s * rows + i, 2 * Z, stride=16), :]
                        to = s * hp + (i * (Y // 2) + t) * (2 * Z)
                        qaug[2 * b + half, to:to + 2 * Z, :] = jnp.concatenate(
                            [qh * first, qh * (1.0 - first)], axis=1).astype(BF16)

    def both(even, odd, g):
        at = pl.ds((g // nb // 2) * bp + g % nb * CHUNK, CHUNK)
        return jnp.concatenate([even[at, :], odd[at, :]], axis=1)

    def score(g):
        s = dot_t(qaug[g // nb], both(k0, k1, g))
        sb[g % 2] = s
        top = s[:, :128]
        for j in range(1, CHUNK // 128):
            top = jnp.maximum(top, s[:, j * 128:(j + 1) * 128])
        cm[g % 2] = top

    def soften(g):
        u, slot = g // nb % 2, g % 2
        m1 = jnp.max(cm[slot], axis=1, keepdims=True) * c2s
        if g % nb:
            m0 = mm[u]
            m1 = jnp.maximum(m0, m1)
            al = jnp.exp2(m0 - m1)
            alb[slot] = al
        else:
            m1 = jnp.broadcast_to(m1, (MOST * hp, 128))
        p = jnp.exp2(sb[slot] * c2s - m1[:, :1])
        ps = p[:, :128]
        for j in range(1, CHUNK // 128):
            ps = ps + p[:, j * 128:(j + 1) * 128]
        ll[u] = ll[u] * al + ps if g % nb else ps
        mm[u] = m1
        pb[slot] = p.astype(BF16)

    def gain(g):
        u, slot = g // nb % 2, g % 2
        o = dot(pb[slot], both(v0, v1, g))
        if g % nb:
            al = alb[slot]
            acc[u] = acc[u] * jnp.concatenate([al, al], axis=1) + o
        else:
            acc[u] = o

    def pack(unit):
        u, b = unit % 2, unit // 2
        places = hp // rows
        ln = lax.broadcasted_iota(jnp.int32, (hp, 128), 1)
        rw = lax.div(lax.broadcasted_iota(jnp.int32, (hp, 128), 0), places)
        stat = jnp.zeros((hp, 128), F32)
        for s in range(MOST):
            sl = pl.ds(s * hp, hp)
            tot = jnp.sum(ll[u, sl, :], axis=1, keepdims=True)
            lse = mm[u, sl, :] + jnp.log2(tot)
            first = own_heads[b][s] < per
            ob[s] = jnp.where(first, acc[u, sl, 0:128], acc[u, sl, 128:256]) * (1.0 / tot)
            hi = lse.astype(BF16).astype(F32)
            mid = (lse - hi).astype(BF16).astype(F32)
            lo = (lse - hi) - mid
            val = jnp.where(ln < 16, hi, jnp.where(ln < 32, mid, lo))
            stat = jnp.where((lax.rem(ln, 16) == s * rows + rw) & (ln < 48), val, stat)
        ob[MOST] = stat
        for s in range(MOST + 1):
            for i in range(rows):
                pf[pl.ds(s * rows + i, places, stride=16), :] = ob[s, i * places:(i + 1) * places, :]
        for t, dy in enumerate(rows_of(unit % 2)):
            of_y = pf[t * 2 * Z * 16:(t + 1) * 2 * Z * 16, :].astype(BF16).reshape(2 * Z, 16, 128)
            pay[b, pl.ds(m.y_of(dy) * (2 * Z), 2 * Z)] = of_y
        if 0 in rows_of(unit % 2):
            recv[b, me] = pay[b, me]

    def give(unit):
        to_all(unit // 2, rows_of(unit % 2), pay, recv, asend, ar)

    prepare(0)
    score(0)
    for g in range(4 * nb + 1):
        if g + 1 == 2 * nb:
            prepare(1)
        if g < 4 * nb:
            soften(g)
        if g >= 1:
            gain(g - 1)
        if g + 1 < 4 * nb:
            score(g + 1)
        if g >= 1 and g % nb == 0:
            pack(g // nb - 1)
            give(g // nb - 1)
        if g == nb:
            g3.core(0, 0, c3)
            for dz in near:
                g3.along_z(dz)
                g3.core(0, dz, c3)
        if g == 3 * nb:
            for dz in [0] + near:
                for dy in range(1, Y):
                    g3.along_y(dy, dz)
                    g3.core(dy, dz, c3)
    g3.core_wait(Y * Z, c3)

    def widenkv(i, _):
        kv32[pl.ds(pl.multiple_of(i * 2 * kvr, 2 * kvr), 2 * kvr), :] = (
            bufkv[lax.div(i, 2 * Z), lax.rem(i, 2 * Z)].astype(F32))
        return 0

    lax.fori_loop(0, n, widenkv, 0)
    kk, vvv = [], []
    for g in range(2):
        kk.append(jnp.concatenate([kv32[pl.ds(2 * i + g, n, stride=2 * kvr), :] for i in range(rows)], axis=0))
        vvv.append(jnp.concatenate([kv32[pl.ds(kvr + 2 * i + g, n, stride=2 * kvr), :] for i in range(rows)], axis=0))
    ks = jnp.concatenate(kk, axis=1).astype(BF16)
    vs = jnp.concatenate(vvv, axis=1).astype(BF16)
    qf = q_ref[...].astype(F32)
    rid = lax.broadcasted_iota(jnp.int32, (qr, 128), 0)
    first = (lax.rem(rid, heads) < per).astype(F32)
    qo = jnp.concatenate([qf * first, qf * (1.0 - first)], axis=1).astype(BF16)
    sc = dot_t(qo, ks) * c2s
    kid = lax.broadcasted_iota(jnp.int32, (qr, np_), 1)
    key_pos = lax.rem(kid, n) * rows + lax.div(kid, n)
    row_pos = me * rows + lax.div(lax.broadcasted_iota(jnp.int32, (qr, np_), 0), heads)
    seen = key_pos <= row_pos
    sc = jnp.where(seen, sc, NEG)
    om = jnp.max(sc, axis=1, keepdims=True)
    ow = jnp.where(seen, jnp.exp2(sc - om), 0.0)
    ot = jnp.sum(ow, axis=1, keepdims=True)
    oo = dot(ow.astype(BF16), vs)
    own_o[...] = jnp.where(first > 0.5, oo[:, 0:128], oo[:, 128:256]) * (1.0 / ot)
    own_l[...] = jnp.broadcast_to(om + jnp.log2(ot), (qr, 128))

    for b in range(2):
        rest_of(b, pay, asend, ar).wait_recv()
        f32s[b * n * 16:(b + 1) * n * 16, :] = recv[b].reshape(n * 16, 128).astype(F32)
    st = sum(f32s[pl.ds(MOST * rows + i, 2 * n, stride=16), :] for i in range(rows))
    st = (st + pltpu.roll(st, 128 - 16, 1)) + pltpu.roll(st, 128 - 32, 1)
    st = st.T
    hid = lax.broadcasted_iota(jnp.int32, (heads, 2 * n), 0)
    for i in range(rows):
        at = pl.ds(i * heads, heads)
        own = own_l[at, 0:1]
        top = own
        xs_ = []
        for s in range(MOST):
            x = jnp.where(hm[s] == hid, st[s * rows + i:s * rows + i + 1, :], NEG)
            xs_.append(x)
            top = jnp.maximum(top, jnp.max(x, axis=1, keepdims=True))
        share = jnp.exp2(own - top)
        den = share
        num = share * own_o[at, :]
        for s in range(MOST):
            wt = jnp.exp2(xs_[s] - top)
            den = den + jnp.sum(wt, axis=1, keepdims=True)
            hi = wt.astype(BF16)
            lo = (wt - hi.astype(F32)).astype(BF16)
            r = f32s[pl.ds(s * rows + i, 2 * n, stride=16), :].astype(BF16)
            two = dot(jnp.concatenate([hi, lo], axis=0), r)
            num = num + (two[0:heads] + two[heads:2 * heads])
        a = (num / den).astype(BF16)
        att_ref[at, :] = a
        buf2[m.y, m.z, at, :] = a

    cut = qr - qr // 4
    g2 = GatherZ(m, buf2, pl.ds(0, cut), one_core, *sems[3:6])
    g4 = GatherY(m, buf2, pl.ds(cut, qr - cut), one_core, *sems[6:9])
    g4.start()
    g2.start()
    for i, dz in enumerate(near):
        g2.along_z(dz)
        if i == min(1, len(near) - 1):
            g4.forward()
    for dz in [0] + near:
        for dy in range(1, Y):
            g2.along_y(dy, dz)
    for dz in near:
        g4.across(dz)
    wcopy.wait()
    wgive.wait()
    share = Z * rows
    for dxs in (far_first(X)[:X // 2], far_first(X)[X // 2:]):
        for t, dx in enumerate(dxs):
            x = lax.rem(kv + dx, X)
            for j in range(Z):
                f32s[(t * Z + j) * qr:(t * Z + j + 1) * qr, :] = buf2[x, j].astype(F32)
        out = jnp.zeros((len(dxs) * share, 256), F32)
        for h in range(0, heads, 2):
            a = jnp.concatenate([f32s[pl.ds(h + e, len(dxs) * share, stride=heads), :] for e in range(2)], axis=1)
            at = slice(h * width, (h + 2) * width)
            out = out + dot(a.astype(BF16), jnp.concatenate([wv[0, at, :], wv[1, at, :]], axis=1))
        for t, dx in enumerate(dxs):
            x = lax.rem(kv + dx, X)
            mine = out[t * share:(t + 1) * share]
            halves = [mine[:, 0:128], mine[:, 128:256]]
            for dc in range(2):
                piece = jnp.where(lax.rem(m.c + dc, 2) == 0, halves[0], halves[1]).astype(BF16)
                if (dx, dc) == (0, 0):
                    part_ref[kv, m.c] = piece
                else:
                    k = 2 * dx + dc - 1
                    xp[k] = piece
                    pltpu.make_async_remote_copy(
                        src_ref=xp.at[k], dst_ref=part_ref.at[kv, m.c], send_sem=xs.at[k], recv_sem=xrs.at[k],
                        device_id=(m.rank(0, 0, dc), x), device_id_type=MESH).start()
    g3.drain(True)
    g2.drain(False)
    g4.drain()
    for b in range(2):
        rest_of(b, qpay, qs, qrs).wait_send()
        rest_of(b, pay, asend, ar).wait_send()
    for dx in range(X):
        for dc in range(2):
            if (dx, dc) != (0, 0):
                k = 2 * dx + dc - 1
                pltpu.make_async_remote_copy(
                    src_ref=xp.at[k], dst_ref=part_ref.at[lax.rem(kv + X - dx, X), lax.rem(m.c + dc, 2)],
                    send_sem=xs.at[k], recv_sem=xrs.at[k],
                    device_id=(m.rank(0, 0, dc), lax.rem(kv + dx, X)), device_id_type=MESH).wait()


def close(att_ref, part_ref, a_ref, p_ref):
    a_ref[...] = att_ref[...]
    rows = p_ref.shape[0]
    sums = []
    for c in range(2):
        total = part_ref[0, c].astype(F32)
        for x in range(1, X):
            total = total + part_ref[x, c].astype(F32)
        sums.append(total.reshape(rows // 16, 8, 128))
    low = lax.broadcasted_iota(jnp.int32, sums[0].shape, 1) < 4
    even = jnp.where(low, sums[0], pltpu.roll(sums[1], 4, 1))
    odd = jnp.where(low, pltpu.roll(sums[0], 4, 1), sums[1])
    p_ref[...] = jnp.stack([even, odd], axis=1).reshape(rows, 128).astype(BF16)


def local(queries, span_keys, span_values, cache_keys, cache_values, gating, out_weight):
    rows, heads, width = queries.shape
    groups = span_keys.shape[1]
    n = Y * Z * 2
    np_ = n * rows
    qr = rows * heads
    kvr = rows * groups
    bp = BLOCK_POSITIONS
    raw = 2 * bp * groups
    part = min(1024, raw // 2)
    unit = MOST * np_ // 2
    vm = pltpu.VMEM
    dma = pltpu.SemaphoreType.DMA
    along_z = [dma((Z - 1,)), dma((Z, Y - 1)), dma((3,))]
    along_y = [dma((Y - 1,)), dma((Z - 1,)), dma((3,))]
    scratch = [
        vm((raw, width), BF16), vm((raw, width), BF16),
        vm((2 * bp, width), BF16), vm((2 * bp, width), BF16), vm((2 * bp, width), BF16), vm((2 * bp, width), BF16),
        vm((2, *out_weight.shape), BF16),
        vm((2, n, 16, width), BF16), vm((2, n, 16, width), BF16), vm((Y, Z, qr, width), BF16), vm((Y, 2 * Z, 2 * kvr, width), BF16),
        vm((n * qr, width), F32), vm((n * 2 * kvr, width), F32), vm((part, width), F32),
        vm((4, unit, 2 * width), BF16),
        vm((2, unit, CHUNK), F32), vm((2, unit, width), F32), vm((2, unit, CHUNK), BF16), vm((2, unit, width), F32),
        vm((2, unit, 2 * width), F32), vm((2, unit, width), F32), vm((2, unit, width), F32),
        vm((MOST + 1, np_ // 2, width), F32), vm((n // 2 * 16, width), F32),
        vm((2, n, 16, width), BF16), vm((2, n, 16, width), BF16),
        vm((qr, width), F32), vm((qr, width), F32),
        vm((2 * X - 1, Z * rows, width), BF16),
        dma((2 * (raw // part),)), dma, dma((2,)), dma, dma((2 * X - 1,)), dma((2 * X - 1,)), dma, dma, dma, dma((2,)), dma,
        *along_z, *along_z, *along_y,
    ]
    inv = pl.BlockSpec(memory_space=pltpu.VMEM)
    anyw = pl.BlockSpec(memory_space=pl.ANY)
    att, parts = pl.pallas_call(
        kernel,
        out_shape=(jax.ShapeDtypeStruct((qr, width), BF16), jax.ShapeDtypeStruct((X, 2, Z * rows, width), BF16)),
        in_specs=[inv, inv, inv, inv, anyw, anyw, anyw],
        out_specs=(inv, inv),
        scratch_shapes=scratch,
        compiler_params=pltpu.CompilerParams(collective_id=0, has_side_effects=True, vmem_limit_bytes=60 << 20),
        name="sparse_attention",
    )(
        queries.reshape(qr, width), span_keys.reshape(kvr, width), span_values.reshape(kvr, width), gating,
        cache_keys.reshape(raw, width), cache_values.reshape(raw, width), out_weight,
    )
    att, proj = pl.pallas_call(
        close,
        out_shape=(jax.ShapeDtypeStruct((qr, width), BF16), jax.ShapeDtypeStruct((np_ // X, width), BF16)),
        in_specs=[inv, inv],
        out_specs=(inv, inv),
        name="close",
    )(att, parts)
    return att.reshape(rows, heads, width), proj


def solution(mesh):
    placed = (
        P("ctx", "kvh", None),
        P("ctx", "kvh", None),
        P("ctx", "kvh", None),
        P("ctx", "kvh", None),
        P("ctx", "kvh", None),
        P("kvh", None),
        P("kvh", "ctx"),
    )
    return jax.shard_map(
        local,
        mesh=mesh,
        in_specs=placed,
        out_specs=(P("ctx", "kvh", None), P("kvh", "ctx")),
        check_vma=False,
    )
```

```python
import functools

import jax
import jax.numpy as jnp
from jax import lax
from jax.experimental import pallas as pl
from jax.experimental.pallas import tpu as pltpu
from jax.sharding import PartitionSpec as P

Y, Z, X = 4, 8, 4
BLOCK_POSITIONS = 4096
MOST = 3
CHUNK = 1024
NEG = -1e30
MESH = pl.DeviceIdType.MESH
F32, BF16 = jnp.float32, jnp.bfloat16


def far_first(n):
    return sorted(range(n), key=lambda d: -min(d, n - d))


def near_first(n):
    return far_first(n)[:-1][::-1]


def dot_t(a, b):
    return lax.dot_general(a, b, (((1,), (1,)), ((), ())), preferred_element_type=F32)


def dot(a, b):
    return jnp.dot(a, b, preferred_element_type=F32)


class Comm:
    def __init__(self):
        self.me = lax.axis_index("ctx")
        self.kv = lax.axis_index("kvh")
        self.c = lax.rem(self.me, 2)
        self.z = lax.rem(lax.div(self.me, 2), Z)
        self.y = lax.div(self.me, 2 * Z)

    def rank(self, dy, dz, dc):
        return (lax.rem(self.y + dy, Y) * Z + lax.rem(self.z + dz, Z)) * 2 + lax.rem(self.c + dc, 2)

    def y_of(self, dy):
        return lax.rem(self.y + dy, Y)

    def copy(self, ref, send, recv, dy, dz, dc):
        return pltpu.make_async_remote_copy(src_ref=ref, dst_ref=ref, send_sem=send, recv_sem=recv,
                                            device_id=(self.rank(dy, dz, dc), self.kv), device_id_type=MESH)


class GatherZ:
    def __init__(self, m, buf, at, slot, zs, ys, sends, ahead=()):
        self.m, self.buf, self.at, self.slot = m, buf, at, slot
        self.zs, self.ys, self.sends = zs, ys, sends
        self.ahead = ahead or far_first(Y)[:-1]

    def ref(self, dy, dz):
        return self.buf.at[self.m.y_of(dy), self.slot(dz), self.at]

    def spread(self, dz):
        m = self.m
        for dy in self.ahead:
            m.copy(self.ref(0, Z - dz), self.sends.at[1], self.ys.at[dz, dy - 1], dy, 0, 0).start()

    def start(self):
        m = self.m
        for dz in near_first(Z):
            m.copy(self.ref(0, 0), self.sends.at[0], self.zs.at[dz - 1], 0, dz, 0).start()
        self.spread(0)

    def along_z(self, dz):
        self.m.copy(self.ref(0, Z - dz), self.sends.at[0], self.zs.at[dz - 1], 0, dz, 0).wait_recv()
        self.spread(dz)

    def along_y(self, dy, dz):
        self.m.copy(self.ref(dy, Z - dz), self.sends.at[1], self.ys.at[dz, Y - dy - 1], Y - dy, 0, 0).wait_recv()

    def core(self, dy, dz, sem):
        self.m.copy(self.ref(dy, Z - dz), self.sends.at[2], sem, 0, 0, 1).start()

    def core_wait(self, number, sem):
        shards = self.buf.at[pl.ds(0, number // Z), pl.ds(0, Z), self.at]
        self.m.copy(shards, self.sends.at[2], sem, 0, 0, 1).wait_recv()

    def drain(self, core):
        m = self.m
        parts = [self.buf.at[0, pl.ds(0, Z - 1), self.at], self.buf.at[pl.ds(0, Y - 1), pl.ds(0, Z), self.at]]
        if core:
            parts.append(self.buf.at[:, pl.ds(0, Z), self.at])
        for i, part in enumerate(parts):
            m.copy(part, self.sends.at[i], self.zs.at[0], 0, 0, 1).wait_send()


class GatherY:
    def __init__(self, m, buf, at, slot, ys, zs, sends):
        self.m, self.buf, self.at, self.slot = m, buf, at, slot
        self.ys, self.zs, self.sends = ys, zs, sends

    def start(self):
        m = self.m
        ref = self.buf.at[m.y, self.slot(0), self.at]
        for dy in far_first(Y)[:-1]:
            m.copy(ref, self.sends.at[0], self.ys.at[dy - 1], dy, 0, 0).start()

    def forward(self):
        m = self.m
        for dy in near_first(Y):
            ref = self.buf.at[m.y_of(Y - dy), self.slot(0), self.at]
            m.copy(ref, self.sends.at[0], self.ys.at[dy - 1], dy, 0, 0).wait_recv()
        for dz in far_first(Z)[:-1]:
            m.copy(self.buf.at[:, self.slot(0), self.at], self.sends.at[1], self.zs.at[dz - 1], 0, dz, 0).start()

    def across(self, dz):
        ref = self.buf.at[:, self.slot(Z - dz), self.at]
        self.m.copy(ref, self.sends.at[1], self.zs.at[dz - 1], 0, dz, 0).wait_recv()

    def drain(self):
        m = self.m
        m.copy(self.buf.at[0, pl.ds(0, Y - 1), self.at], self.sends.at[0], self.zs.at[0], 0, 0, 1).wait_send()
        m.copy(self.buf.at[:, pl.ds(0, Z - 1), self.at], self.sends.at[1], self.zs.at[0], 0, 0, 1).wait_send()


def kernel(q_ref, sk_ref, sv_ref, gat_ref, kc_ref, vc_ref, w_ref, att_ref, part_ref,
           kraw, vraw, k0, k1, v0, v1, wv, buf, buf2, bufkv, f32s, kv32, d32, qaug,
           sb, cm, pb, alb, acc, mm, ll, ob, pf, pay, recv, own_o, own_l, xp,
           loc, wl, ar, asend, xs, xrs, ws, wrs, c1, c3, *sems):
    m = Comm()
    zc = 2 * m.z + m.c

    def both_cores(dz):
        return 2 * lax.rem(m.z + dz, Z) + m.c

    def one_core(dz):
        return lax.rem(m.z + dz, Z)

    n = Y * Z * 2
    me, kv = m.me, m.kv
    heads, topk = gat_ref.shape
    rows = q_ref.shape[0] // heads
    per = heads // 2
    width = q_ref.shape[1]
    bp = BLOCK_POSITIONS
    np_ = n * rows
    qr = rows * heads
    kvr = sk_ref.shape[0]
    row = 2 * Z * rows
    hp = Y // 2 * row
    c2s = width ** -0.5 * 1.4426950408889634

    wcopy = pltpu.make_async_copy(w_ref, wv.at[m.c], wl)
    wgive = pltpu.make_async_remote_copy(src_ref=w_ref, dst_ref=wv.at[m.c], send_sem=ws, recv_sem=wrs,
                                         device_id=(m.rank(0, 0, 1), kv), device_id_type=MESH)
    bar = pltpu.get_barrier_semaphore()
    for dz in far_first(Z)[:-1]:
        pl.semaphore_signal(bar, inc=1, device_id=(m.rank(0, dz, 0), kv), device_id_type=MESH)
    for dy in far_first(Y)[:-1]:
        pl.semaphore_signal(bar, inc=1, device_id=(m.rank(dy, 0, 0), kv), device_id_type=MESH)
    for dx in range(X):
        for dc in range(2):
            if (dx, dc) != (0, 0):
                pl.semaphore_signal(bar, inc=1, device_id=(m.rank(0, 0, dc), lax.rem(kv + dx, X)), device_id_type=MESH)
    buf[m.y, zc] = q_ref[...]
    bufkv[m.y, zc] = jnp.concatenate([sk_ref[...], sv_ref[...]], axis=0)

    lane = lax.broadcasted_iota(jnp.int32, (heads, 2 * n), 1)
    block_of = lax.rem(lane, n) * 2 + lax.div(lane, n)
    gat = gat_ref[...]
    chosen = jnp.zeros((heads, 2 * n), jnp.int32)
    for t in range(topk):
        chosen = jnp.maximum(chosen, (gat[:, t:t + 1] == block_of).astype(jnp.int32))
    count = jnp.zeros((1, 2 * n), jnp.int32)
    hm = [jnp.full((1, 2 * n), -1, jnp.int32) for _ in range(MOST)]
    for h in range(heads):
        ch = chosen[h:h + 1, :]
        for s in range(MOST):
            hm[s] = jnp.where((ch == 1) & (count == s), h, hm[s])
        count = count + ch
    lane1 = lax.broadcasted_iota(jnp.int32, (1, 2 * n), 1)
    own_heads = [[jnp.maximum(jnp.max(jnp.where(lane1 == b * n + me, hm[s], -1)), 0) for s in range(MOST)]
                 for b in range(2)]

    part = d32.shape[0]
    parts = kraw.shape[0] // part
    order = [(a, blk * (parts // 2) + i) for blk in range(2) for a in range(2) for i in range(parts // 2)]
    arrays = ((kc_ref, kraw, k0, k1), (vc_ref, vraw, v0, v1))

    def load(j):
        a, i = order[j]
        at = pl.ds(i * part, part)
        return pltpu.make_async_copy(arrays[a][0].at[at], arrays[a][1].at[at], loc.at[j])

    def pieces():
        for j, (a, i) in enumerate(order):
            load(j).wait()
            _, raw, even, odd = arrays[a]
            to = pl.ds(i * (part // 2), part // 2)
            d32[...] = raw[pl.ds(i * part, part), :].astype(F32)
            even[to, :] = d32[pl.ds(0, part // 2, stride=2), :].astype(BF16)
            odd[to, :] = d32[pl.ds(1, part // 2, stride=2), :].astype(BF16)
            yield

    work = pieces()

    def beside(number):
        for _ in range(number):
            next(work, None)

    for j in range(len(order)):
        load(j).start()
    beside(2)
    pl.semaphore_wait(bar, Z - 1 + Y - 1 + 2 * X - 1)

    near = near_first(Z)
    g1 = GatherZ(m, buf, pl.ds(0, qr), both_cores, sems[0], sems[1], sems[2], ahead=range(Y - 1, 0, -1))
    g1.start()
    g1.core(0, 0, c1.at[0])
    beside(len(order) * 3 // 8)
    for dz in near:
        g1.along_z(dz)
        g1.core(0, dz, c1.at[0])
    first_half = list(range(1, Y // 2))
    second_half = list(range(Y // 2, Y))
    beside(len(order) * 3 // 8)
    for dz in [0] + near:
        for dy in first_half:
            g1.along_y(dy, dz)
            g1.core(dy, dz, c1.at[0])
    beside(len(order))
    wcopy.start()
    g1.core_wait(Y * Z // 2, c1.at[0])
    wgive.start()
    g3 = GatherZ(m, bufkv, pl.ds(0, 2 * kvr), both_cores, sems[3], sems[4], sems[5])
    g3.start()

    nb = bp // CHUNK

    def rows_of(half):
        return list(range(half * (Y // 2), (half + 1) * (Y // 2)))

    def prepare(half):
        for dy in rows_of(half):
            yy = m.y_of(dy)
            f32s[pl.ds(yy * (2 * Z * qr), 2 * Z * qr), :] = buf[yy].reshape(2 * Z * qr, 128).astype(F32)
        for b in range(2):
            for s in range(MOST):
                h = own_heads[b][s]
                first = (h < per).astype(F32)
                for i in range(rows):
                    for t, dy in enumerate(rows_of(half)):
                        qh = f32s[pl.ds(m.y_of(dy) * (row * heads) + i * heads + h, 2 * Z, stride=qr), :]
                        to = s * hp + (i * (Y // 2) + t) * (2 * Z)
                        qaug[2 * half + b, to:to + 2 * Z, :] = jnp.concatenate(
                            [qh * first, qh * (1.0 - first)], axis=1).astype(BF16)

    def both(even, odd, g):
        at = pl.ds((g // nb % 2) * bp + g % nb * CHUNK, CHUNK)
        return jnp.concatenate([even[at, :], odd[at, :]], axis=1)

    def score(g):
        s = dot_t(qaug[g // nb], both(k0, k1, g))
        sb[g % 2] = s
        top = s[:, :128]
        for j in range(1, CHUNK // 128):
            top = jnp.maximum(top, s[:, j * 128:(j + 1) * 128])
        cm[g % 2] = top

    def soften(g):
        u, slot = g // nb % 2, g % 2
        m1 = jnp.max(cm[slot], axis=1, keepdims=True) * c2s
        if g % nb:
            m0 = mm[u]
            m1 = jnp.maximum(m0, m1)
            al = jnp.exp2(m0 - m1)
            alb[slot] = al
        else:
            m1 = jnp.broadcast_to(m1, (MOST * hp, 128))
        p = jnp.exp2(sb[slot] * c2s - m1[:, :1])
        ps = p[:, :128]
        for j in range(1, CHUNK // 128):
            ps = ps + p[:, j * 128:(j + 1) * 128]
        ll[u] = ll[u] * al + ps if g % nb else ps
        mm[u] = m1
        pb[slot] = p.astype(BF16)

    def gain(g):
        u, slot = g // nb % 2, g % 2
        o = dot(pb[slot], both(v0, v1, g))
        if g % nb:
            al = alb[slot]
            acc[u] = acc[u] * jnp.concatenate([al, al], axis=1) + o
        else:
            acc[u] = o

    def pack(unit):
        u, b = unit % 2, unit % 2
        places = hp // rows
        ln = lax.broadcasted_iota(jnp.int32, (hp, 128), 1)
        rw = lax.div(lax.broadcasted_iota(jnp.int32, (hp, 128), 0), places)
        stat = jnp.zeros((hp, 128), F32)
        for s in range(MOST):
            sl = pl.ds(s * hp, hp)
            tot = jnp.sum(ll[u, sl, :], axis=1, keepdims=True)
            lse = mm[u, sl, :] + jnp.log2(tot)
            first = own_heads[b][s] < per
            ob[s] = jnp.where(first, acc[u, sl, 0:128], acc[u, sl, 128:256]) * (1.0 / tot)
            hi = lse.astype(BF16).astype(F32)
            mid = (lse - hi).astype(BF16).astype(F32)
            lo = (lse - hi) - mid
            val = jnp.where(ln < 16, hi, jnp.where(ln < 32, mid, lo))
            stat = jnp.where((lax.rem(ln, 16) == s * rows + rw) & (ln < 48), val, stat)
        ob[MOST] = stat
        for s in range(MOST + 1):
            for i in range(rows):
                pf[pl.ds(s * rows + i, places, stride=16), :] = ob[s, i * places:(i + 1) * places, :]
        for t, dy in enumerate(rows_of(unit // 2)):
            of_y = pf[t * 2 * Z * 16:(t + 1) * 2 * Z * 16, :].astype(BF16).reshape(2 * Z, 16, 128)
            pay[b, pl.ds(m.y_of(dy) * (2 * Z), 2 * Z)] = of_y
        if unit // 2 == 0:
            recv[b, me] = pay[b, me]

    def give(unit):
        b = unit % 2
        dys = rows_of(unit // 2)

        def send(dy, dz, dc):
            to = m.rank(dy, dz, dc)
            pltpu.make_async_remote_copy(src_ref=pay.at[b, to], dst_ref=recv.at[b, me], send_sem=asend,
                                         recv_sem=ar.at[b], device_id=(to, kv), device_id_type=MESH).start()

        def sends(i, _):
            k = lax.div(i + 1, 2)
            dz = Z // 2 + jnp.where(lax.rem(i, 2) == 1, -k, k)
            for dy in dys:
                for dc in range(2):
                    send(dy, dz, dc)
            return 0

        lax.fori_loop(0, Z - 1, sends, 0)
        for dy in dys:
            for dc in range(2):
                if (dy, dc) != (0, 0):
                    send(dy, 0, dc)

    prepare(0)
    score(0)
    for g in range(4 * nb + 1):
        if g + 1 == 2 * nb:
            g1.core_wait(Y * Z // 2, c1.at[1])
            prepare(1)
        if g < 4 * nb:
            soften(g)
        if g >= 1:
            gain(g - 1)
        if g + 1 < 4 * nb:
            score(g + 1)
        if g >= 1 and g % nb == 0:
            pack(g // nb - 1)
            give(g // nb - 1)
        if g == nb - 1:
            for dz in [0] + near:
                for dy in second_half:
                    g1.along_y(dy, dz)
                    g1.core(dy, dz, c1.at[1])
        if g == 2 * nb:
            g3.core(0, 0, c3)
            for dz in near:
                g3.along_z(dz)
                g3.core(0, dz, c3)
    for dz in [0] + near:
        for dy in range(1, Y):
            g3.along_y(dy, dz)
            g3.core(dy, dz, c3)
    g3.core_wait(Y * Z, c3)

    kv32[...] = bufkv[...].reshape(n * 2 * kvr, 128).astype(F32)
    kk, vvv = [], []
    for g in range(2):
        kk.append(jnp.concatenate([kv32[pl.ds(2 * i + g, n, stride=2 * kvr), :] for i in range(rows)], axis=0))
        vvv.append(jnp.concatenate([kv32[pl.ds(kvr + 2 * i + g, n, stride=2 * kvr), :] for i in range(rows)], axis=0))
    ks = jnp.concatenate(kk, axis=1).astype(BF16)
    vs = jnp.concatenate(vvv, axis=1).astype(BF16)
    qf = q_ref[...].astype(F32)
    rid = lax.broadcasted_iota(jnp.int32, (qr, 128), 0)
    first = (lax.rem(rid, heads) < per).astype(F32)
    qo = jnp.concatenate([qf * first, qf * (1.0 - first)], axis=1).astype(BF16)
    sc = dot_t(qo, ks) * c2s
    kid = lax.broadcasted_iota(jnp.int32, (qr, np_), 1)
    key_pos = lax.rem(kid, n) * rows + lax.div(kid, n)
    row_pos = me * rows + lax.div(lax.broadcasted_iota(jnp.int32, (qr, np_), 0), heads)
    seen = key_pos <= row_pos
    sc = jnp.where(seen, sc, NEG)
    om = jnp.max(sc, axis=1, keepdims=True)
    ow = jnp.where(seen, jnp.exp2(sc - om), 0.0)
    ot = jnp.sum(ow, axis=1, keepdims=True)
    oo = dot(ow.astype(BF16), vs)
    own_o[...] = jnp.where(first > 0.5, oo[:, 0:128], oo[:, 128:256]) * (1.0 / ot)
    own_l[...] = jnp.broadcast_to(om + jnp.log2(ot), (qr, 128))

    for b in range(2):
        rest = pay.at[b, pl.ds(0, n - 1)]
        pltpu.make_async_remote_copy(src_ref=rest, dst_ref=rest, send_sem=asend, recv_sem=ar.at[b],
                                     device_id=(m.rank(0, 1, 0), kv), device_id_type=MESH).wait_recv()
        f32s[b * n * 16:(b + 1) * n * 16, :] = recv[b].reshape(n * 16, 128).astype(F32)
    st = sum(f32s[pl.ds(MOST * rows + i, 2 * n, stride=16), :] for i in range(rows))
    st = (st + pltpu.roll(st, 128 - 16, 1)) + pltpu.roll(st, 128 - 32, 1)
    st = st.T
    hid = lax.broadcasted_iota(jnp.int32, (heads, 2 * n), 0)
    for i in range(rows):
        at = pl.ds(i * heads, heads)
        own = own_l[at, 0:1]
        top = own
        xs_ = []
        for s in range(MOST):
            x = jnp.where(hm[s] == hid, st[s * rows + i:s * rows + i + 1, :], NEG)
            xs_.append(x)
            top = jnp.maximum(top, jnp.max(x, axis=1, keepdims=True))
        share = jnp.exp2(own - top)
        den = share
        num = share * own_o[at, :]
        for s in range(MOST):
            wt = jnp.exp2(xs_[s] - top)
            den = den + jnp.sum(wt, axis=1, keepdims=True)
            hi = wt.astype(BF16)
            lo = (wt - hi.astype(F32)).astype(BF16)
            r = f32s[pl.ds(s * rows + i, 2 * n, stride=16), :].astype(BF16)
            two = dot(jnp.concatenate([hi, lo], axis=0), r)
            num = num + (two[0:heads] + two[heads:2 * heads])
        a = (num / den).astype(BF16)
        att_ref[at, :] = a
        buf2[m.y, m.z, at, :] = a

    cut = qr - qr // 4
    g2 = GatherZ(m, buf2, pl.ds(0, cut), one_core, *sems[6:9])
    g4 = GatherY(m, buf2, pl.ds(cut, qr - cut), one_core, *sems[9:12])
    g4.start()
    g2.start()
    for i, dz in enumerate(near):
        g2.along_z(dz)
        if i == min(1, len(near) - 1):
            g4.forward()
    for dz in [0] + near:
        for dy in range(1, Y):
            g2.along_y(dy, dz)
    for dz in near:
        g4.across(dz)
    wcopy.wait()
    wgive.wait()
    share = Z * rows
    for dxs in (far_first(X)[:X // 2], far_first(X)[X // 2:]):
        for t, dx in enumerate(dxs):
            x = lax.rem(kv + dx, X)
            for j in range(Z):
                f32s[(t * Z + j) * qr:(t * Z + j + 1) * qr, :] = buf2[x, j].astype(F32)
        out = jnp.zeros((len(dxs) * share, 256), F32)
        for h in range(0, heads, 2):
            a = jnp.concatenate([f32s[pl.ds(h + e, len(dxs) * share, stride=heads), :] for e in range(2)], axis=1)
            at = slice(h * width, (h + 2) * width)
            out = out + dot(a.astype(BF16), jnp.concatenate([wv[0, at, :], wv[1, at, :]], axis=1))
        for t, dx in enumerate(dxs):
            x = lax.rem(kv + dx, X)
            mine = out[t * share:(t + 1) * share]
            halves = [mine[:, 0:128], mine[:, 128:256]]
            for dc in range(2):
                piece = jnp.where(lax.rem(m.c + dc, 2) == 0, halves[0], halves[1]).astype(BF16)
                if (dx, dc) == (0, 0):
                    part_ref[kv, m.c] = piece
                else:
                    k = 2 * dx + dc - 1
                    xp[k] = piece
                    pltpu.make_async_remote_copy(
                        src_ref=xp.at[k], dst_ref=part_ref.at[kv, m.c], send_sem=xs.at[k], recv_sem=xrs.at[k],
                        device_id=(m.rank(0, 0, dc), x), device_id_type=MESH).start()
    g1.drain(True)
    g3.drain(True)
    g2.drain(False)
    g4.drain()
    for b in range(2):
        rest = pay.at[b, pl.ds(0, n - 1)]
        pltpu.make_async_remote_copy(src_ref=rest, dst_ref=rest, send_sem=asend, recv_sem=ar.at[b],
                                     device_id=(m.rank(0, 1, 0), kv), device_id_type=MESH).wait_send()
    for dx in range(X):
        for dc in range(2):
            if (dx, dc) != (0, 0):
                k = 2 * dx + dc - 1
                pltpu.make_async_remote_copy(
                    src_ref=xp.at[k], dst_ref=part_ref.at[lax.rem(kv + X - dx, X), lax.rem(m.c + dc, 2)],
                    send_sem=xs.at[k], recv_sem=xrs.at[k],
                    device_id=(m.rank(0, 0, dc), lax.rem(kv + dx, X)), device_id_type=MESH).wait()


def close(att_ref, part_ref, a_ref, p_ref):
    a_ref[...] = att_ref[...]
    rows = p_ref.shape[0]
    sums = []
    for c in range(2):
        total = part_ref[0, c].astype(F32)
        for x in range(1, X):
            total = total + part_ref[x, c].astype(F32)
        sums.append(total.reshape(rows // 16, 8, 128))
    low = lax.broadcasted_iota(jnp.int32, sums[0].shape, 1) < 4
    even = jnp.where(low, sums[0], pltpu.roll(sums[1], 4, 1))
    odd = jnp.where(low, pltpu.roll(sums[0], 4, 1), sums[1])
    p_ref[...] = jnp.stack([even, odd], axis=1).reshape(rows, 128).astype(BF16)


def local(queries, span_keys, span_values, cache_keys, cache_values, gating, out_weight):
    rows, heads, width = queries.shape
    groups = span_keys.shape[1]
    n = Y * Z * 2
    np_ = n * rows
    qr = rows * heads
    kvr = rows * groups
    bp = BLOCK_POSITIONS
    raw = 2 * bp * groups
    part = min(1024, raw // 2)
    unit = MOST * np_ // 2
    vm = pltpu.VMEM
    dma = pltpu.SemaphoreType.DMA
    along_z = [dma((Z - 1,)), dma((Z, Y - 1)), dma((3,))]
    along_y = [dma((Y - 1,)), dma((Z - 1,)), dma((3,))]
    scratch = [
        vm((raw, width), BF16), vm((raw, width), BF16),
        vm((2 * bp, width), BF16), vm((2 * bp, width), BF16), vm((2 * bp, width), BF16), vm((2 * bp, width), BF16),
        vm((2, *out_weight.shape), BF16),
        vm((Y, 2 * Z, qr, width), BF16), vm((Y, Z, qr, width), BF16), vm((Y, 2 * Z, 2 * kvr, width), BF16),
        vm((n * qr, width), F32), vm((n * 2 * kvr, width), F32), vm((part, width), F32),
        vm((4, unit, 2 * width), BF16),
        vm((2, unit, CHUNK), F32), vm((2, unit, width), F32), vm((2, unit, CHUNK), BF16), vm((2, unit, width), F32),
        vm((2, unit, 2 * width), F32), vm((2, unit, width), F32), vm((2, unit, width), F32),
        vm((MOST + 1, np_ // 2, width), F32), vm((n // 2 * 16, width), F32),
        vm((2, n, 16, width), BF16), vm((2, n, 16, width), BF16),
        vm((qr, width), F32), vm((qr, width), F32),
        vm((2 * X - 1, Z * rows, width), BF16),
        dma((2 * (raw // part),)), dma, dma((2,)), dma, dma((2 * X - 1,)), dma((2 * X - 1,)), dma, dma, dma((2,)), dma,
        *along_z, *along_z, *along_z, *along_y,
    ]
    inv = pl.BlockSpec(memory_space=pltpu.VMEM)
    anyw = pl.BlockSpec(memory_space=pl.ANY)
    att, parts = pl.pallas_call(
        kernel,
        out_shape=(jax.ShapeDtypeStruct((qr, width), BF16), jax.ShapeDtypeStruct((X, 2, Z * rows, width), BF16)),
        in_specs=[inv, inv, inv, inv, anyw, anyw, anyw],
        out_specs=(inv, inv),
        scratch_shapes=scratch,
        compiler_params=pltpu.CompilerParams(collective_id=0, has_side_effects=True, vmem_limit_bytes=60 << 20),
        name="sparse_attention",
    )(
        queries.reshape(qr, width), span_keys.reshape(kvr, width), span_values.reshape(kvr, width), gating,
        cache_keys.reshape(raw, width), cache_values.reshape(raw, width), out_weight,
    )
    att, proj = pl.pallas_call(
        close,
        out_shape=(jax.ShapeDtypeStruct((qr, width), BF16), jax.ShapeDtypeStruct((np_ // X, width), BF16)),
        in_specs=[inv, inv],
        out_specs=(inv, inv),
        name="close",
    )(att, parts)
    return att.reshape(rows, heads, width), proj


def solution(mesh):
    placed = (
        P("ctx", "kvh", None),
        P("ctx", "kvh", None),
        P("ctx", "kvh", None),
        P("ctx", "kvh", None),
        P("ctx", "kvh", None),
        P("kvh", None),
        P("kvh", "ctx"),
    )
    return jax.shard_map(
        local,
        mesh=mesh,
        in_specs=placed,
        out_specs=(P("ctx", "kvh", None), P("kvh", "ctx")),
        check_vma=False,
    )
```

```python
import functools

import jax
import jax.numpy as jnp
from jax import lax
from jax.experimental import pallas as pl
from jax.experimental.pallas import tpu as pltpu
from jax.sharding import PartitionSpec as P

Y, Z, X = 4, 8, 4
BLOCK_POSITIONS = 4096
MOST = 3
CHUNK = 1024
NEG = -1e30
MESH = pl.DeviceIdType.MESH
F32, BF16 = jnp.float32, jnp.bfloat16


def far_first(n):
    return sorted(range(n), key=lambda d: -min(d, n - d))


def near_first(n):
    return far_first(n)[:-1][::-1]


def dot_t(a, b):
    return lax.dot_general(a, b, (((1,), (1,)), ((), ())), preferred_element_type=F32)


def dot(a, b):
    return jnp.dot(a, b, preferred_element_type=F32)


class Comm:
    def __init__(self):
        self.me = lax.axis_index("ctx")
        self.kv = lax.axis_index("kvh")
        self.c = lax.rem(self.me, 2)
        self.z = lax.rem(lax.div(self.me, 2), Z)
        self.y = lax.div(self.me, 2 * Z)

    def rank(self, dy, dz, dc):
        return (lax.rem(self.y + dy, Y) * Z + lax.rem(self.z + dz, Z)) * 2 + lax.rem(self.c + dc, 2)

    def y_of(self, dy):
        return lax.rem(self.y + dy, Y)

    def copy(self, ref, send, recv, dy, dz, dc):
        return pltpu.make_async_remote_copy(src_ref=ref, dst_ref=ref, send_sem=send, recv_sem=recv,
                                            device_id=(self.rank(dy, dz, dc), self.kv), device_id_type=MESH)


class GatherZ:
    def __init__(self, m, buf, at, slot, zs, ys, sends, ahead=()):
        self.m, self.buf, self.at, self.slot = m, buf, at, slot
        self.zs, self.ys, self.sends = zs, ys, sends
        self.ahead = ahead or far_first(Y)[:-1]

    def ref(self, dy, dz):
        return self.buf.at[self.m.y_of(dy), self.slot(dz), self.at]

    def spread(self, dz):
        m = self.m
        for dy in self.ahead:
            m.copy(self.ref(0, Z - dz), self.sends.at[1], self.ys.at[dz, dy - 1], dy, 0, 0).start()

    def start(self):
        m = self.m
        for dz in near_first(Z):
            m.copy(self.ref(0, 0), self.sends.at[0], self.zs.at[dz - 1], 0, dz, 0).start()
        self.spread(0)

    def along_z(self, dz):
        self.m.copy(self.ref(0, Z - dz), self.sends.at[0], self.zs.at[dz - 1], 0, dz, 0).wait_recv()
        self.spread(dz)

    def along_y(self, dy, dz):
        self.m.copy(self.ref(dy, Z - dz), self.sends.at[1], self.ys.at[dz, Y - dy - 1], Y - dy, 0, 0).wait_recv()

    def core(self, dy, dz, sem):
        self.m.copy(self.ref(dy, Z - dz), self.sends.at[2], sem, 0, 0, 1).start()

    def core_wait(self, number, sem):
        shards = self.buf.at[pl.ds(0, number // Z), pl.ds(0, Z), self.at]
        self.m.copy(shards, self.sends.at[2], sem, 0, 0, 1).wait_recv()

    def drain(self, core):
        m = self.m
        parts = [self.buf.at[0, pl.ds(0, Z - 1), self.at], self.buf.at[pl.ds(0, Y - 1), pl.ds(0, Z), self.at]]
        if core:
            parts.append(self.buf.at[:, pl.ds(0, Z), self.at])
        for i, part in enumerate(parts):
            m.copy(part, self.sends.at[i], self.zs.at[0], 0, 0, 1).wait_send()


class GatherY:
    def __init__(self, m, buf, at, slot, ys, zs, sends):
        self.m, self.buf, self.at, self.slot = m, buf, at, slot
        self.ys, self.zs, self.sends = ys, zs, sends

    def start(self):
        m = self.m
        ref = self.buf.at[m.y, self.slot(0), self.at]
        for dy in far_first(Y)[:-1]:
            m.copy(ref, self.sends.at[0], self.ys.at[dy - 1], dy, 0, 0).start()

    def forward(self):
        m = self.m
        for dy in near_first(Y):
            ref = self.buf.at[m.y_of(Y - dy), self.slot(0), self.at]
            m.copy(ref, self.sends.at[0], self.ys.at[dy - 1], dy, 0, 0).wait_recv()
        for dz in far_first(Z)[:-1]:
            m.copy(self.buf.at[:, self.slot(0), self.at], self.sends.at[1], self.zs.at[dz - 1], 0, dz, 0).start()

    def across(self, dz):
        ref = self.buf.at[:, self.slot(Z - dz), self.at]
        self.m.copy(ref, self.sends.at[1], self.zs.at[dz - 1], 0, dz, 0).wait_recv()

    def drain(self):
        m = self.m
        m.copy(self.buf.at[0, pl.ds(0, Y - 1), self.at], self.sends.at[0], self.zs.at[0], 0, 0, 1).wait_send()
        m.copy(self.buf.at[:, pl.ds(0, Z - 1), self.at], self.sends.at[1], self.zs.at[0], 0, 0, 1).wait_send()


def kernel(q_ref, sk_ref, sv_ref, gat_ref, kc_ref, vc_ref, w_ref, att_ref, part_ref,
           kraw, vraw, k0, k1, v0, v1, wv, buf, buf2, bufkv, f32s, kv32, d32, qaug,
           sb, cm, pb, alb, acc, mm, ll, ob, pf, pay, recv, own_o, own_l, xp,
           loc, wl, ar, asend, xs, xrs, ws, wrs, c1, c3, *sems):
    m = Comm()
    zc = 2 * m.z + m.c

    def both_cores(dz):
        return 2 * lax.rem(m.z + dz, Z) + m.c

    def one_core(dz):
        return lax.rem(m.z + dz, Z)

    n = Y * Z * 2
    me, kv = m.me, m.kv
    heads, topk = gat_ref.shape
    rows = q_ref.shape[0] // heads
    per = heads // 2
    width = q_ref.shape[1]
    bp = BLOCK_POSITIONS
    np_ = n * rows
    qr = rows * heads
    kvr = sk_ref.shape[0]
    row = 2 * Z * rows
    hp = Y // 2 * row
    c2s = width ** -0.5 * 1.4426950408889634

    wcopy = pltpu.make_async_copy(w_ref, wv.at[m.c], wl)
    wgive = pltpu.make_async_remote_copy(src_ref=w_ref, dst_ref=wv.at[m.c], send_sem=ws, recv_sem=wrs,
                                         device_id=(m.rank(0, 0, 1), kv), device_id_type=MESH)
    bar = pltpu.get_barrier_semaphore()
    for dz in far_first(Z)[:-1]:
        pl.semaphore_signal(bar, inc=1, device_id=(m.rank(0, dz, 0), kv), device_id_type=MESH)
    for dy in far_first(Y)[:-1]:
        pl.semaphore_signal(bar, inc=1, device_id=(m.rank(dy, 0, 0), kv), device_id_type=MESH)
    for dx in range(X):
        for dc in range(2):
            if (dx, dc) != (0, 0):
                pl.semaphore_signal(bar, inc=1, device_id=(m.rank(0, 0, dc), lax.rem(kv + dx, X)), device_id_type=MESH)
    buf[m.y, zc] = q_ref[...]
    bufkv[m.y, zc] = jnp.concatenate([sk_ref[...], sv_ref[...]], axis=0)

    part = d32.shape[0]
    parts = kraw.shape[0] // part
    order = [(a, blk * (parts // 2) + i) for blk in range(2) for a in range(2) for i in range(parts // 2)]
    arrays = ((kc_ref, kraw, k0, k1), (vc_ref, vraw, v0, v1))

    def load(j):
        a, i = order[j]
        at = pl.ds(i * part, part)
        return pltpu.make_async_copy(arrays[a][0].at[at], arrays[a][1].at[at], loc.at[j])

    def pieces():
        for j, (a, i) in enumerate(order):
            load(j).wait()
            _, raw, even, odd = arrays[a]
            to = pl.ds(i * (part // 2), part // 2)
            d32[...] = raw[pl.ds(i * part, part), :].astype(F32)
            even[to, :] = d32[pl.ds(0, part // 2, stride=2), :].astype(BF16)
            odd[to, :] = d32[pl.ds(1, part // 2, stride=2), :].astype(BF16)
            yield

    work = pieces()

    def beside(number):
        for _ in range(number):
            next(work, None)

    for j in range(len(order)):
        load(j).start()
    pl.semaphore_wait(bar, Z - 1 + Y - 1 + 2 * X - 1)

    near = near_first(Z)
    g1 = GatherZ(m, buf, pl.ds(0, qr), both_cores, sems[0], sems[1], sems[2], ahead=range(Y - 1, 0, -1))
    g1.start()
    g1.core(0, 0, c1.at[0])

    lane = lax.broadcasted_iota(jnp.int32, (heads, 2 * n), 1)
    block_of = lax.rem(lane, n) * 2 + lax.div(lane, n)
    gat = gat_ref[...]
    chosen = jnp.zeros((heads, 2 * n), jnp.int32)
    for t in range(topk):
        chosen = jnp.maximum(chosen, (gat[:, t:t + 1] == block_of).astype(jnp.int32))
    count = jnp.zeros((1, 2 * n), jnp.int32)
    hm = [jnp.full((1, 2 * n), -1, jnp.int32) for _ in range(MOST)]
    for h in range(heads):
        ch = chosen[h:h + 1, :]
        for s in range(MOST):
            hm[s] = jnp.where((ch == 1) & (count == s), h, hm[s])
        count = count + ch
    lane1 = lax.broadcasted_iota(jnp.int32, (1, 2 * n), 1)
    own_heads = [[jnp.maximum(jnp.max(jnp.where(lane1 == b * n + me, hm[s], -1)), 0) for s in range(MOST)]
                 for b in range(2)]

    beside(len(order) * 3 // 8)
    for dz in near:
        g1.along_z(dz)
        g1.core(0, dz, c1.at[0])
    first_half = list(range(1, Y // 2))
    second_half = list(range(Y // 2, Y))
    beside(len(order) * 3 // 8)
    for dz in [0] + near:
        for dy in first_half:
            g1.along_y(dy, dz)
            g1.core(dy, dz, c1.at[0])
    beside(len(order))
    wcopy.start()
    g1.core_wait(Y * Z // 2, c1.at[0])
    wgive.start()
    g3 = GatherZ(m, bufkv, pl.ds(0, 2 * kvr), both_cores, sems[3], sems[4], sems[5])
    g3.start()

    nb = bp // CHUNK

    def rows_of(half):
        return list(range(half * (Y // 2), (half + 1) * (Y // 2)))

    def prepare(half):
        for dy in rows_of(half):
            yy = m.y_of(dy)
            f32s[pl.ds(yy * (2 * Z * qr), 2 * Z * qr), :] = buf[yy].reshape(2 * Z * qr, 128).astype(F32)
        for b in range(2):
            for s in range(MOST):
                h = own_heads[b][s]
                first = (h < per).astype(F32)
                for i in range(rows):
                    for t, dy in enumerate(rows_of(half)):
                        qh = f32s[pl.ds(m.y_of(dy) * (row * heads) + i * heads + h, 2 * Z, stride=qr), :]
                        to = s * hp + (i * (Y // 2) + t) * (2 * Z)
                        qaug[2 * half + b, to:to + 2 * Z, :] = jnp.concatenate(
                            [qh * first, qh * (1.0 - first)], axis=1).astype(BF16)

    def both(even, odd, g):
        at = pl.ds((g // nb % 2) * bp + g % nb * CHUNK, CHUNK)
        return jnp.concatenate([even[at, :], odd[at, :]], axis=1)

    def score(g):
        s = dot_t(qaug[g // nb], both(k0, k1, g))
        sb[g % 2] = s
        top = s[:, :128]
        for j in range(1, CHUNK // 128):
            top = jnp.maximum(top, s[:, j * 128:(j + 1) * 128])
        cm[g % 2] = top

    def soften(g):
        u, slot = g // nb % 2, g % 2
        m1 = jnp.max(cm[slot], axis=1, keepdims=True) * c2s
        if g % nb:
            m0 = mm[u]
            m1 = jnp.maximum(m0, m1)
            al = jnp.exp2(m0 - m1)
            alb[slot] = al
        else:
            m1 = jnp.broadcast_to(m1, (MOST * hp, 128))
        p = jnp.exp2(sb[slot] * c2s - m1[:, :1])
        ps = p[:, :128]
        for j in range(1, CHUNK // 128):
            ps = ps + p[:, j * 128:(j + 1) * 128]
        ll[u] = ll[u] * al + ps if g % nb else ps
        mm[u] = m1
        pb[slot] = p.astype(BF16)

    def gain(g):
        u, slot = g // nb % 2, g % 2
        o = dot(pb[slot], both(v0, v1, g))
        if g % nb:
            al = alb[slot]
            acc[u] = acc[u] * jnp.concatenate([al, al], axis=1) + o
        else:
            acc[u] = o

    def pack(unit):
        u, b = unit % 2, unit % 2
        places = hp // rows
        ln = lax.broadcasted_iota(jnp.int32, (hp, 128), 1)
        rw = lax.div(lax.broadcasted_iota(jnp.int32, (hp, 128), 0), places)
        stat = jnp.zeros((hp, 128), F32)
        for s in range(MOST):
            sl = pl.ds(s * hp, hp)
            tot = jnp.sum(ll[u, sl, :], axis=1, keepdims=True)
            lse = mm[u, sl, :] + jnp.log2(tot)
            first = own_heads[b][s] < per
            ob[s] = jnp.where(first, acc[u, sl, 0:128], acc[u, sl, 128:256]) * (1.0 / tot)
            hi = lse.astype(BF16).astype(F32)
            mid = (lse - hi).astype(BF16).astype(F32)
            lo = (lse - hi) - mid
            val = jnp.where(ln < 16, hi, jnp.where(ln < 32, mid, lo))
            stat = jnp.where((lax.rem(ln, 16) == s * rows + rw) & (ln < 48), val, stat)
        ob[MOST] = stat
        for s in range(MOST + 1):
            for i in range(rows):
                pf[pl.ds(s * rows + i, places, stride=16), :] = ob[s, i * places:(i + 1) * places, :]
        for t, dy in enumerate(rows_of(unit // 2)):
            of_y = pf[t * 2 * Z * 16:(t + 1) * 2 * Z * 16, :].astype(BF16).reshape(2 * Z, 16, 128)
            pay[b, pl.ds(m.y_of(dy) * (2 * Z), 2 * Z)] = of_y
        if unit // 2 == 0:
            recv[b, me] = pay[b, me]

    def give(unit):
        b = unit % 2
        dys = rows_of(unit // 2)

        def send(dy, dz, dc):
            to = m.rank(dy, dz, dc)
            pltpu.make_async_remote_copy(src_ref=pay.at[b, to], dst_ref=recv.at[b, me], send_sem=asend,
                                         recv_sem=ar.at[b], device_id=(to, kv), device_id_type=MESH).start()

        def sends(i, _):
            k = lax.div(i + 1, 2)
            dz = Z // 2 + jnp.where(lax.rem(i, 2) == 1, -k, k)
            for dy in dys:
                for dc in range(2):
                    send(dy, dz, dc)
            return 0

        lax.fori_loop(0, Z - 1, sends, 0)
        for dy in dys:
            for dc in range(2):
                if (dy, dc) != (0, 0):
                    send(dy, 0, dc)

    prepare(0)
    score(0)
    for g in range(4 * nb + 1):
        if g + 1 == 2 * nb:
            g1.core_wait(Y * Z // 2, c1.at[1])
            prepare(1)
        if g < 4 * nb:
            soften(g)
        if g >= 1:
            gain(g - 1)
        if g + 1 < 4 * nb:
            score(g + 1)
        if g >= 1 and g % nb == 0:
            pack(g // nb - 1)
            give(g // nb - 1)
        if g == nb - 1:
            for dz in [0] + near:
                for dy in second_half:
                    g1.along_y(dy, dz)
                    g1.core(dy, dz, c1.at[1])
        if g == 2 * nb:
            g3.core(0, 0, c3)
            for dz in near:
                g3.along_z(dz)
                g3.core(0, dz, c3)
    for dz in [0] + near:
        for dy in range(1, Y):
            g3.along_y(dy, dz)
            g3.core(dy, dz, c3)
    g3.core_wait(Y * Z, c3)

    kv32[...] = bufkv[...].reshape(n * 2 * kvr, 128).astype(F32)
    kk, vvv = [], []
    for g in range(2):
        kk.append(jnp.concatenate([kv32[pl.ds(2 * i + g, n, stride=2 * kvr), :] for i in range(rows)], axis=0))
        vvv.append(jnp.concatenate([kv32[pl.ds(kvr + 2 * i + g, n, stride=2 * kvr), :] for i in range(rows)], axis=0))
    ks = jnp.concatenate(kk, axis=1).astype(BF16)
    vs = jnp.concatenate(vvv, axis=1).astype(BF16)
    qf = q_ref[...].astype(F32)
    rid = lax.broadcasted_iota(jnp.int32, (qr, 128), 0)
    first = (lax.rem(rid, heads) < per).astype(F32)
    qo = jnp.concatenate([qf * first, qf * (1.0 - first)], axis=1).astype(BF16)
    sc = dot_t(qo, ks) * c2s
    kid = lax.broadcasted_iota(jnp.int32, (qr, np_), 1)
    key_pos = lax.rem(kid, n) * rows + lax.div(kid, n)
    row_pos = me * rows + lax.div(lax.broadcasted_iota(jnp.int32, (qr, np_), 0), heads)
    seen = key_pos <= row_pos
    sc = jnp.where(seen, sc, NEG)
    om = jnp.max(sc, axis=1, keepdims=True)
    ow = jnp.where(seen, jnp.exp2(sc - om), 0.0)
    ot = jnp.sum(ow, axis=1, keepdims=True)
    oo = dot(ow.astype(BF16), vs)
    own_o[...] = jnp.where(first > 0.5, oo[:, 0:128], oo[:, 128:256]) * (1.0 / ot)
    own_l[...] = jnp.broadcast_to(om + jnp.log2(ot), (qr, 128))

    for b in range(2):
        rest = pay.at[b, pl.ds(0, n - 1)]
        pltpu.make_async_remote_copy(src_ref=rest, dst_ref=rest, send_sem=asend, recv_sem=ar.at[b],
                                     device_id=(m.rank(0, 1, 0), kv), device_id_type=MESH).wait_recv()
        f32s[b * n * 16:(b + 1) * n * 16, :] = recv[b].reshape(n * 16, 128).astype(F32)
    st = sum(f32s[pl.ds(MOST * rows + i, 2 * n, stride=16), :] for i in range(rows))
    st = (st + pltpu.roll(st, 128 - 16, 1)) + pltpu.roll(st, 128 - 32, 1)
    st = st.T
    hid = lax.broadcasted_iota(jnp.int32, (heads, 2 * n), 0)
    for i in range(rows):
        at = pl.ds(i * heads, heads)
        own = own_l[at, 0:1]
        top = own
        xs_ = []
        for s in range(MOST):
            x = jnp.where(hm[s] == hid, st[s * rows + i:s * rows + i + 1, :], NEG)
            xs_.append(x)
            top = jnp.maximum(top, jnp.max(x, axis=1, keepdims=True))
        share = jnp.exp2(own - top)
        den = share
        num = share * own_o[at, :]
        for s in range(MOST):
            wt = jnp.exp2(xs_[s] - top)
            den = den + jnp.sum(wt, axis=1, keepdims=True)
            hi = wt.astype(BF16)
            lo = (wt - hi.astype(F32)).astype(BF16)
            r = f32s[pl.ds(s * rows + i, 2 * n, stride=16), :].astype(BF16)
            two = dot(jnp.concatenate([hi, lo], axis=0), r)
            num = num + (two[0:heads] + two[heads:2 * heads])
        a = (num / den).astype(BF16)
        att_ref[at, :] = a
        buf2[m.y, m.z, at, :] = a

    cut = qr - qr // 4
    g2 = GatherZ(m, buf2, pl.ds(0, cut), one_core, *sems[6:9])
    g4 = GatherY(m, buf2, pl.ds(cut, qr - cut), one_core, *sems[9:12])
    g4.start()
    g2.start()
    for i, dz in enumerate(near):
        g2.along_z(dz)
        if i == min(1, len(near) - 1):
            g4.forward()
    for dz in [0] + near:
        for dy in range(1, Y):
            g2.along_y(dy, dz)
    for dz in near:
        g4.across(dz)
    wcopy.wait()
    wgive.wait()
    share = Z * rows
    for dxs in (far_first(X)[:X // 2], far_first(X)[X // 2:]):
        for t, dx in enumerate(dxs):
            x = lax.rem(kv + dx, X)
            for j in range(Z):
                f32s[(t * Z + j) * qr:(t * Z + j + 1) * qr, :] = buf2[x, j].astype(F32)
        out = jnp.zeros((len(dxs) * share, 256), F32)
        for h in range(0, heads, 2):
            a = jnp.concatenate([f32s[pl.ds(h + e, len(dxs) * share, stride=heads), :] for e in range(2)], axis=1)
            at = slice(h * width, (h + 2) * width)
            out = out + dot(a.astype(BF16), jnp.concatenate([wv[0, at, :], wv[1, at, :]], axis=1))
        for t, dx in enumerate(dxs):
            x = lax.rem(kv + dx, X)
            mine = out[t * share:(t + 1) * share]
            halves = [mine[:, 0:128], mine[:, 128:256]]
            for dc in range(2):
                piece = jnp.where(lax.rem(m.c + dc, 2) == 0, halves[0], halves[1]).astype(BF16)
                if (dx, dc) == (0, 0):
                    part_ref[kv, m.c] = piece
                else:
                    k = 2 * dx + dc - 1
                    xp[k] = piece
                    pltpu.make_async_remote_copy(
                        src_ref=xp.at[k], dst_ref=part_ref.at[kv, m.c], send_sem=xs.at[k], recv_sem=xrs.at[k],
                        device_id=(m.rank(0, 0, dc), x), device_id_type=MESH).start()
    g1.drain(True)
    g3.drain(True)
    g2.drain(False)
    g4.drain()
    for b in range(2):
        rest = pay.at[b, pl.ds(0, n - 1)]
        pltpu.make_async_remote_copy(src_ref=rest, dst_ref=rest, send_sem=asend, recv_sem=ar.at[b],
                                     device_id=(m.rank(0, 1, 0), kv), device_id_type=MESH).wait_send()
    for dx in range(X):
        for dc in range(2):
            if (dx, dc) != (0, 0):
                k = 2 * dx + dc - 1
                pltpu.make_async_remote_copy(
                    src_ref=xp.at[k], dst_ref=part_ref.at[lax.rem(kv + X - dx, X), lax.rem(m.c + dc, 2)],
                    send_sem=xs.at[k], recv_sem=xrs.at[k],
                    device_id=(m.rank(0, 0, dc), lax.rem(kv + dx, X)), device_id_type=MESH).wait()


def close(att_ref, part_ref, a_ref, p_ref):
    a_ref[...] = att_ref[...]
    rows = p_ref.shape[0]
    sums = []
    for c in range(2):
        total = part_ref[0, c].astype(F32)
        for x in range(1, X):
            total = total + part_ref[x, c].astype(F32)
        sums.append(total.reshape(rows // 16, 8, 128))
    low = lax.broadcasted_iota(jnp.int32, sums[0].shape, 1) < 4
    even = jnp.where(low, sums[0], pltpu.roll(sums[1], 4, 1))
    odd = jnp.where(low, pltpu.roll(sums[0], 4, 1), sums[1])
    p_ref[...] = jnp.stack([even, odd], axis=1).reshape(rows, 128).astype(BF16)


def local(queries, span_keys, span_values, cache_keys, cache_values, gating, out_weight):
    rows, heads, width = queries.shape
    groups = span_keys.shape[1]
    n = Y * Z * 2
    np_ = n * rows
    qr = rows * heads
    kvr = rows * groups
    bp = BLOCK_POSITIONS
    raw = 2 * bp * groups
    part = min(1024, raw // 2)
    unit = MOST * np_ // 2
    vm = pltpu.VMEM
    dma = pltpu.SemaphoreType.DMA
    along_z = [dma((Z - 1,)), dma((Z, Y - 1)), dma((3,))]
    along_y = [dma((Y - 1,)), dma((Z - 1,)), dma((3,))]
    scratch = [
        vm((raw, width), BF16), vm((raw, width), BF16),
        vm((2 * bp, width), BF16), vm((2 * bp, width), BF16), vm((2 * bp, width), BF16), vm((2 * bp, width), BF16),
        vm((2, *out_weight.shape), BF16),
        vm((Y, 2 * Z, qr, width), BF16), vm((Y, Z, qr, width), BF16), vm((Y, 2 * Z, 2 * kvr, width), BF16),
        vm((n * qr, width), F32), vm((n * 2 * kvr, width), F32), vm((part, width), F32),
        vm((4, unit, 2 * width), BF16),
        vm((2, unit, CHUNK), F32), vm((2, unit, width), F32), vm((2, unit, CHUNK), BF16), vm((2, unit, width), F32),
        vm((2, unit, 2 * width), F32), vm((2, unit, width), F32), vm((2, unit, width), F32),
        vm((MOST + 1, np_ // 2, width), F32), vm((n // 2 * 16, width), F32),
        vm((2, n, 16, width), BF16), vm((2, n, 16, width), BF16),
        vm((qr, width), F32), vm((qr, width), F32),
        vm((2 * X - 1, Z * rows, width), BF16),
        dma((2 * (raw // part),)), dma, dma((2,)), dma, dma((2 * X - 1,)), dma((2 * X - 1,)), dma, dma, dma((2,)), dma,
        *along_z, *along_z, *along_z, *along_y,
    ]
    inv = pl.BlockSpec(memory_space=pltpu.VMEM)
    anyw = pl.BlockSpec(memory_space=pl.ANY)
    att, parts = pl.pallas_call(
        kernel,
        out_shape=(jax.ShapeDtypeStruct((qr, width), BF16), jax.ShapeDtypeStruct((X, 2, Z * rows, width), BF16)),
        in_specs=[inv, inv, inv, inv, anyw, anyw, anyw],
        out_specs=(inv, inv),
        scratch_shapes=scratch,
        compiler_params=pltpu.CompilerParams(collective_id=0, has_side_effects=True, vmem_limit_bytes=60 << 20),
        name="sparse_attention",
    )(
        queries.reshape(qr, width), span_keys.reshape(kvr, width), span_values.reshape(kvr, width), gating,
        cache_keys.reshape(raw, width), cache_values.reshape(raw, width), out_weight,
    )
    att, proj = pl.pallas_call(
        close,
        out_shape=(jax.ShapeDtypeStruct((qr, width), BF16), jax.ShapeDtypeStruct((np_ // X, width), BF16)),
        in_specs=[inv, inv],
        out_specs=(inv, inv),
        name="close",
    )(att, parts)
    return att.reshape(rows, heads, width), proj


def solution(mesh):
    placed = (
        P("ctx", "kvh", None),
        P("ctx", "kvh", None),
        P("ctx", "kvh", None),
        P("ctx", "kvh", None),
        P("ctx", "kvh", None),
        P("kvh", None),
        P("kvh", "ctx"),
    )
    return jax.shard_map(
        local,
        mesh=mesh,
        in_specs=placed,
        out_specs=(P("ctx", "kvh", None), P("kvh", "ctx")),
        check_vma=False,
    )
```
